128 devices in a mesh: row: 8 (over z, core), col: 16 (over x, y).
Axes of the slice: x: 4, y: 4, z: 4, core: 2. Of those that a mesh axis runs over, the one named last changes fastest.
Arguments:
- cotangent: bfloat16 [524288, 128], P(('row', 'col')), may hold values from -0.0625 to 0.0625
- owner_row: int32 [524288], P(('row', 'col')), may hold values from 0 to 7, as said below
- owner_slot: int32 [524288], P(('row', 'col')), may hold values from 0 to 1535, as said below
- counts: int32 [128], P(('row', 'col')), may hold values from 1 to 1536, as said below
- unique_ids: int32 [196608], P(('row', 'col')), may hold values from 0 to 4194303
- hash_seeds: int32 [3, 1024], replicated, may hold values from 1 to 32767
- w_in: bfloat16 [1024, 1024], replicated, may hold values from -0.1875 to 0.1875
- w_mid: bfloat16 [1024, 1024], replicated, may hold values from -0.1875 to 0.1875
- w_out: bfloat16 [1024, 128], replicated, may hold values from -0.1875 to 0.1875
Outputs:
- grad_in: float32 [1024, 1024], P(('row', 'col'))
- grad_mid: float32 [1024, 1024], P(('row', 'col'))
- grad_out: float32 [1024, 128], P(('row', 'col'))
The draws below stay inside these ranges and needn't reach their ends.
Inputs may be any that keep to these rules, and one draw needn't show every extreme that they name: `owner_row`: A device sends at most 1536 lookups to one owner and exactly 1536 to one owner of its column; all devices of a column send equally many lookups to a given owner. `owner_slot`: A lookup's slot is below the count of its owner (the device at row owner_row in the lookup's column). The counts of the 8 devices of one column sum to 4096, and one device of each column has 1536.
All inputs are finite; a program needn't handle non-finite values.
Results may differ from the reference program's by a relative error of at most 0.0058.
Values may be sent and summed in bfloat16 or wider, within the bound.
No kernel may reach another device: no remote copies, remote signals or barrier semaphores. Data moves between devices by JAX's collectives and lax.ppermute only.
A program may use at most 128 MiB of HBM per device.

```python
import jax
import jax.numpy as jnp
from jax import lax

HASHES = 1024
HIDDEN_SIZE = 1024
EMBED = 128
UNIQUE = 512
SLOTS = 1536
LOOKUPS = 4096
CAPACITY = 1536
N_ROW = 8
N_COL = 16
DEVICES = 128


def layout(key):
    key_hot, key_noise, key_extra, key_order = jax.random.split(key, 4)
    row_axis = jnp.arange(N_ROW, dtype=jnp.int32)[:, None]
    hot_rows = jax.random.randint(key_hot, (1, N_COL), 0, N_ROW, dtype=jnp.int32)
    rest_total = N_ROW * UNIQUE - SLOTS
    base_count = rest_total // (N_ROW - 1)
    remain = rest_total - base_count * (N_ROW - 1)
    spread = max(base_count // 3, 1)
    is_hot = row_axis == hot_rows
    other_rank = row_axis - (row_axis > hot_rows).astype(jnp.int32)
    noise = jax.random.randint(key_noise, (N_ROW - 1, N_COL), 0, spread, dtype=jnp.int32)
    shifts = noise - jnp.roll(noise, 1, axis=0)
    shift_full = jnp.take_along_axis(shifts, jnp.clip(other_rank, 0, N_ROW - 2), axis=0)
    grid = jnp.where(is_hot, SLOTS, base_count + (other_rank < remain).astype(jnp.int32) + shift_full)
    sends = jnp.where(is_hot, CAPACITY, LOOKUPS * grid // (N_ROW * UNIQUE))
    leftover = LOOKUPS - jnp.sum(sends, axis=0, keepdims=True)
    sends = sends + ((other_rank < leftover) & jnp.logical_not(is_hot)).astype(jnp.int32)
    device = jnp.arange(DEVICES, dtype=jnp.int32)
    dev_row = device // N_COL
    dev_col = device % N_COL
    per_dest = sends.T[dev_col]
    count_dest = grid.T[dev_col]
    ends = jnp.cumsum(per_dest, axis=1)
    starts = ends - per_dest
    position = jnp.arange(LOOKUPS, dtype=jnp.int32)
    dest = jnp.sum((position[None, :, None] >= ends[:, None, :]).astype(jnp.int32), axis=2)
    within = position[None, :] - jnp.take_along_axis(starts, dest, axis=1)
    dest_sends = jnp.take_along_axis(per_dest, dest, axis=1)
    dest_count = jnp.take_along_axis(count_dest, dest, axis=1)
    joint = dev_row[:, None] * dest_sends + within
    extra = jax.random.randint(key_extra, (DEVICES, LOOKUPS), 0, dest_count, dtype=jnp.int32)
    slots_drawn = jnp.where(joint < dest_count, joint, extra)
    orders = jax.vmap(lambda one_key: jax.random.permutation(one_key, LOOKUPS))(jax.random.split(key_order, DEVICES))
    owners = jnp.take_along_axis(dest, orders, axis=1)
    slot_values = jnp.take_along_axis(slots_drawn, orders, axis=1)
    return (grid.reshape(-1).astype(jnp.int32), owners.reshape(-1).astype(jnp.int32), slot_values.reshape(-1).astype(jnp.int32))


def draw_owner_row(key, part):
    return layout(key)[1]


def draw_owner_slot(key, part):
    return layout(key)[2]


def draw_counts(key, part):
    return layout(key)[0]


def draw_unique_ids(key, part):
    key = jax.random.fold_in(key, 7)
    span = 4194304 // N_ROW
    dev_row = jnp.arange(DEVICES, dtype=jnp.int32)[:, None] // N_COL
    low_end = dev_row * span
    drawn = jax.random.randint(key, (DEVICES, SLOTS), low_end, low_end + span, dtype=jnp.int32)
    flat = drawn.reshape(-1)
    flat = flat.at[0].set(0)
    return flat.at[(N_ROW - 1) * N_COL * SLOTS].set(N_ROW * span - 1)


def touch_ends(entries, key, low, largest):
    index_at = [jax.random.randint(jax.random.fold_in(key, axis), (), 0, length) for axis, length in enumerate(entries.shape)]
    main_axis = entries.shape.index(max(entries.shape))
    neighbour = index_at[:main_axis] + [(index_at[main_axis] + 1) % entries.shape[main_axis]] + index_at[main_axis + 1:]
    return entries.at[tuple(index_at)].set(low).at[tuple(neighbour)].set(largest)


def steps_of(own_key, dims, cuts, least, high):
    def one(dim, blocks):
        draws = jax.random.uniform(jax.random.fold_in(jax.random.fold_in(own_key, 6), dim), (blocks,), jnp.float32, least / len(cuts), high / len(cuts))
        return jnp.repeat(jnp.exp(draws), dims[dim] // blocks).reshape((-1,) + (1,) * (len(dims) - dim - 1))

    loudness = one(*cuts[0])
    for cut in cuts[1:]:
        loudness = loudness * one(*cut)
    return loudness


def bell_draw(stream_key, extent, width, limit, cuts=(), held_as=jnp.bfloat16):
    values = width * jax.random.normal(stream_key, extent, jnp.float32)
    if cuts:
        values = values * steps_of(stream_key, extent, cuts, -0.22, 0.18)
    return jnp.clip(values, -limit, limit).astype(held_as)


def setup_inputs(seed: int = 0) -> dict:
    keys = jax.random.split(jax.random.key(seed), 10)
    return {
        "cotangent": bell_draw(keys[0], (LOOKUPS * DEVICES, EMBED), (LOOKUPS * DEVICES // 64) ** -0.5, 0.0625, ((0, 128),)),
        "owner_row": draw_owner_row(jax.random.fold_in(keys[9], 71), 0),
        "owner_slot": draw_owner_slot(jax.random.fold_in(keys[9], 71), 0),
        "counts": draw_counts(jax.random.fold_in(keys[9], 71), 0),
        "unique_ids": draw_unique_ids(jax.random.fold_in(keys[9], 71), 0),
        "hash_seeds": touch_ends(jax.random.randint(keys[5], (3, HASHES), 1, 32768), jax.random.fold_in(keys[5], 1), 1, 32767).astype(jnp.int32),
        "w_in": bell_draw(keys[6], (HASHES, HIDDEN_SIZE), HASHES ** -0.5, 0.1875),
        "w_mid": bell_draw(keys[7], (HIDDEN_SIZE, HIDDEN_SIZE), HIDDEN_SIZE ** -0.5, 0.1875),
        "w_out": bell_draw(keys[8], (HIDDEN_SIZE, EMBED), HIDDEN_SIZE ** -0.5, 0.1875),
    }


def hash_encode(id_values, hash_seeds):
    low_part = id_values % 65521
    high_part = (id_values // 65521) % 32749
    first = (low_part[:, None] * hash_seeds[0][None, :]) % 65521
    second = (high_part[:, None] * hash_seeds[1][None, :]) % 65521
    codes = (first + second + hash_seeds[2][None, :]) % 65521
    return (codes.astype(jnp.float32) * (2.0 / 65520.0) - 1.0).astype(jnp.bfloat16)


def mish_parts(pre_act):
    soft = jax.nn.softplus(pre_act)
    tanh_soft = jnp.tanh(soft)
    value = pre_act * tanh_soft
    slope = tanh_soft + pre_act * (1.0 - tanh_soft * tanh_soft) * jax.nn.sigmoid(pre_act)
    return value, slope


def outer_sum(left, right):
    return lax.dot_general(left, right, (((0,), (0,)), ((), ())), preferred_element_type=jnp.float32)


def inner_rows(left, right):
    return lax.dot_general(left, right, (((1,), (1,)), ((), ())), preferred_element_type=jnp.float32)


def local_terms(encoded, grad_use, w_in, w_mid, w_out):
    pre_one = jnp.dot(encoded, w_in, preferred_element_type=jnp.float32)
    act_one, slope_one = mish_parts(pre_one)
    act_one = act_one.astype(jnp.bfloat16)
    pre_two = jnp.dot(act_one, w_mid, preferred_element_type=jnp.float32)
    act_two, slope_two = mish_parts(pre_two)
    act_two = act_two.astype(jnp.bfloat16)
    grad_out = outer_sum(act_two, grad_use)
    delta_two = (inner_rows(grad_use, w_out) * slope_two).astype(jnp.bfloat16)
    grad_mid = outer_sum(act_one, delta_two)
    delta_one = (inner_rows(delta_two, w_mid) * slope_one).astype(jnp.bfloat16)
    grad_in = outer_sum(encoded, delta_one)
    return grad_in, grad_mid, grad_out


def reference(cotangent, owner_row, owner_slot, counts, unique_ids, hash_seeds, w_in, w_mid, w_out):
    grid = counts.reshape(N_ROW, N_COL)
    before = jnp.cumsum(grid, axis=0) - grid
    column_base = (jnp.arange(N_COL, dtype=jnp.int32) * (N_ROW * UNIQUE))[None, :] + before
    live_total = DEVICES * UNIQUE
    column = (jnp.arange(DEVICES * LOOKUPS, dtype=jnp.int32) // LOOKUPS) % N_COL
    target = column_base[owner_row, column] + owner_slot
    sums = jax.ops.segment_sum(cotangent.astype(jnp.float32), target, num_segments=live_total)
    grad_use = sums.astype(jnp.bfloat16)
    slot_axis = jnp.arange(SLOTS, dtype=jnp.int32)
    live_mask = slot_axis[None, :] < counts[:, None]
    places = jnp.where(live_mask, column_base.reshape(-1)[:, None] + slot_axis[None, :], live_total)
    compact = jnp.zeros((live_total,), jnp.int32).at[places.reshape(-1)].set(unique_ids, mode="drop")
    id_blocks = compact.reshape(DEVICES, UNIQUE)
    grad_blocks = grad_use.reshape(DEVICES, UNIQUE, EMBED)
    initial = (jnp.zeros((HASHES, HIDDEN_SIZE), jnp.float32), jnp.zeros((HIDDEN_SIZE, HIDDEN_SIZE), jnp.float32),
               jnp.zeros((HIDDEN_SIZE, EMBED), jnp.float32))

    def accumulate(carry, block):
        terms = local_terms(hash_encode(block[0], hash_seeds), block[1], w_in, w_mid, w_out)
        return (carry[0] + terms[0], carry[1] + terms[1], carry[2] + terms[2]), None

    totals, _ = lax.scan(accumulate, initial, (id_blocks, grad_blocks))
    return totals[0], totals[1], totals[2]
```

```python
import jax
import jax.numpy as jnp
from jax import lax
from jax.experimental import pallas as pl
from jax.experimental.pallas import tpu as pltpu
from jax.sharding import Mesh, PartitionSpec as P

PRIME = 65521
HIGH_PRIME = 32749
SLOTS = 1536
LOOKUPS = 4096
WIDTH = 1024
EMBED = 128
ALL = ("z", "core", "x", "y")
VMEM_LIMIT = 56 * 1024 * 1024
BF16 = jnp.bfloat16
F32 = jnp.float32
I32 = jnp.int32


def vmem(count):
    return [pl.BlockSpec(memory_space=pltpu.VMEM)] * count


def params(**extra):
    return pltpu.CompilerParams(vmem_limit_bytes=VMEM_LIMIT, **extra)


def owner_ranges(table_ref):
    first = jnp.zeros((1, 1), I32)
    ranges = []
    for owner in range(8):
        count = table_ref[owner * 16 + 12 : owner * 16 + 13, 0:1]
        ranges.append((first, count))
        first = first + count
    return ranges


def segment_kernel(me_ref, table_ref, row_ref, slot_ref, cot_ref, keep_ref, send_ref, wide, hot):
    z, core = me_ref[0], me_ref[1]
    owner = row_ref[...]
    place = slot_ref[...]
    for index, (first, _) in enumerate(owner_ranges(table_ref)):
        place = jnp.where(owner == index, place + first, place)
    place = place ^ (core << 9)
    quarter = ((place >> 10) - z) & 3
    inner = place & 1023
    quarter_t = quarter.T
    for chunk in range(32):
        rows = slice(chunk * 128, chunk * 128 + 128)
        column = jnp.broadcast_to(quarter_t[:, chunk : chunk + 1], (128, 128))
        cot = cot_ref[rows, :].astype(F32)
        for part in range(4):
            wide[rows, part * 128 : part * 128 + 128] = jnp.where(column == part, cot, 0.0).astype(BF16)
    for half in (1, 0):
        ids = lax.broadcasted_iota(I32, (512, 128), 0) + half * 512
        for chunk in range(32):
            hit = inner[chunk : chunk + 1, :] == ids
            hot[:, chunk * 128 : chunk * 128 + 128] = jnp.where(hit, 1.0, 0.0).astype(BF16)
        for pair in range(2):
            total = jnp.dot(hot[...], wide[:, pair * 256 : pair * 256 + 256], preferred_element_type=F32)
            for sub in range(2):
                part = pair * 2 + sub
                rows = slice(part * 512, part * 512 + 512)
                piece = total[:, sub * 128 : sub * 128 + 128]
                if half:
                    send_ref[rows, :] = piece.astype(BF16)
                else:
                    keep_ref[rows, :] = piece


def join_kernel(keep_ref, got_ref, own_ref, one_ref, two_ref, three_ref):
    own_ref[...] = keep_ref[0:512, :] + got_ref[0:512, :].astype(F32)
    for part, out in enumerate((one_ref, two_ref, three_ref), 1):
        rows = slice(part * 512, part * 512 + 512)
        out[...] = (keep_ref[rows, :] + got_ref[rows, :].astype(F32)).astype(BF16)


def total_kernel(own_ref, one_ref, two_ref, three_ref, after_ref, out_ref):
    total = own_ref[...] + one_ref[...].astype(F32) + two_ref[...].astype(F32) + three_ref[...].astype(F32)
    out_ref[...] = total.astype(BF16)


def mish_parts(value):
    e = jnp.exp(jnp.minimum(value, 20.0))
    n = e * (e + 2.0)
    inverse = 1.0 / (n + 2.0)
    tanh_soft = n * inverse
    act = value * tanh_soft
    slope = tanh_soft + act_term(value, e) * (inverse * inverse)
    return act, slope


def act_term(value, e):
    return value * (4.0 * (e * (e + 1.0)))


def forward_kernel(me_ref, table_ref, after_ref, seeds_ref, w_in_ref, w_mid_ref,
                   slope_one_ref, slope_two_ref, enc_t_ref, one_t_ref, two_t_ref,
                   enc, one, two):
    z, core = me_ref[0], me_ref[1]
    block = pl.program_id(0)
    line = lax.broadcasted_iota(I32, (256, 1), 0) + block * 256
    place = z * 1024 + (line ^ (core << 9))
    where_at = jnp.zeros((256, 1), I32)
    for index, (first, count) in enumerate(owner_ranges(table_ref)):
        inside = (place >= first) & (place < first + count)
        where_at = jnp.where(inside, place - first + index * 2048, where_at)
    lane = lax.broadcasted_iota(I32, (256, 128), 1)
    pick = jnp.where((where_at >> 7) == lane, 1.0, 0.0).astype(BF16)
    table = table_ref[...]
    bytes_of = jnp.concatenate(
        [(table & 255).astype(F32), ((table >> 8) & 255).astype(F32), (table >> 16).astype(F32)], axis=1
    ).astype(BF16)
    found = jnp.dot(pick, bytes_of, preferred_element_type=F32)
    found = found[:, 0:128] + 256.0 * found[:, 128:256] + 65536.0 * found[:, 256:384]
    found = jnp.sum(jnp.where((where_at & 127) == lane, found, 0.0), axis=1, keepdims=True).astype(I32)
    low = (found >> 16) * 15 + (found & 65535)
    over = low >= PRIME
    high = (found >> 16) + jnp.where(over, 1, 0)
    low = jnp.where(over, low - PRIME, low)
    high = jnp.where(high >= HIGH_PRIME, high - HIGH_PRIME, high)
    for step in range(4):
        cols = slice(step * 256, step * 256 + 256)
        mix = low * seeds_ref[0:1, cols] + (high * seeds_ref[1:2, cols] + seeds_ref[2:3, cols])
        mix = lax.shift_right_logical(mix, 16) * 15 + (mix & 65535)
        mix = (mix >> 16) * 15 + (mix & 65535)
        mix = jnp.where(mix >= PRIME, mix - PRIME, mix)
        enc[:, cols] = (mix.astype(F32) * (2.0 / 65520.0) - 1.0).astype(BF16)
    for step in range(4):
        cols = slice(step * 256, step * 256 + 256)
        act, slope = mish_parts(jnp.dot(enc[...], w_in_ref[:, cols], preferred_element_type=F32))
        one[:, cols] = act.astype(BF16)
        slope_one_ref[:, cols] = slope.astype(slope_one_ref.dtype)
    for step in range(4):
        cols = slice(step * 256, step * 256 + 256)
        act, slope = mish_parts(jnp.dot(one[...], w_mid_ref[:, cols], preferred_element_type=F32))
        two[:, cols] = act.astype(BF16)
        slope_two_ref[:, cols] = slope.astype(slope_two_ref.dtype)
    for part in range(4):
        cols = pl.ds(pl.multiple_of(core * 128 + part * 256, 128), 128)
        rows = slice(part * 128, part * 128 + 128)
        for source, out in ((enc, enc_t_ref), (one, one_t_ref), (two, two_t_ref)):
            out[rows, :] = source[:, cols].T


def backward_kernel(mine_ref, other_ref, slope_one_ref, slope_two_ref, enc_t_ref, one_t_ref, two_t_ref,
                    w_mid_ref, w_out_ref, out_ref, total, delta_two, delta_one):
    step = pl.program_id(0)
    nt = (((1,), (1,)), ((), ()))

    @pl.when(step == 0)
    def _():
        total[...] = jnp.zeros_like(total)

    rows = pl.ds(pl.multiple_of((step % 2) * 256, 256), 256)
    grad = jnp.where(step < 2, mine_ref[rows, :].astype(F32), other_ref[rows, :].astype(F32)).astype(BF16)
    for part in range(4):
        cols = slice(part * 256, part * 256 + 256)
        back = lax.dot_general(grad, w_out_ref[cols, :], nt, preferred_element_type=F32)
        delta_two[:, cols] = (back * slope_two_ref[:, cols].astype(F32)).astype(BF16)
    for part in range(4):
        cols = slice(part * 256, part * 256 + 256)
        back = lax.dot_general(delta_two[...], w_mid_ref[cols, :], nt, preferred_element_type=F32)
        delta_one[:, cols] = (back * slope_one_ref[:, cols].astype(F32)).astype(BF16)
    total[:, 2048:2176] += jnp.dot(two_t_ref[...], grad, preferred_element_type=F32)
    for part in range(4):
        cols = slice(part * 256, part * 256 + 256)
        total[:, 1024 + part * 256 : 1280 + part * 256] += jnp.dot(
            one_t_ref[...], delta_two[:, cols], preferred_element_type=F32)
        total[:, cols] += jnp.dot(enc_t_ref[...], delta_one[:, cols], preferred_element_type=F32)

    @pl.when(step == 3)
    def _():
        out_ref[...] = total[...].astype(BF16)


def shift(steps):
    return [(index, (index + steps) % 4) for index in range(4)]


SWAP = [(0, 1), (1, 0)]


def per_device(cotangent, owner_row, owner_slot, counts, unique_ids, hash_seeds, w_in, w_mid, w_out):
    shape = jax.ShapeDtypeStruct
    smem = pl.BlockSpec(memory_space=pltpu.SMEM)
    me = jnp.stack([lax.axis_index("z"), lax.axis_index("core")]).astype(I32)

    with jax.named_scope("gather_ids"):
        own_table = jnp.concatenate(
            [unique_ids.reshape(12, 128), jnp.broadcast_to(counts.reshape(1, 1), (4, 128))], axis=0)
        copies = jnp.broadcast_to(own_table[None], (8, 16, 128))
        table = lax.all_to_all(copies, ("z", "core"), split_axis=0, concat_axis=0, tiled=True).reshape(128, 128)

    keep, send = pl.pallas_call(
        segment_kernel,
        out_shape=(shape((2048, EMBED), F32), shape((2048, EMBED), BF16)),
        in_specs=[smem] + vmem(4),
        out_specs=tuple(vmem(2)),
        scratch_shapes=[pltpu.VMEM((LOOKUPS, 512), BF16), pltpu.VMEM((512, LOOKUPS), BF16)],
        compiler_params=params(),
        cost_estimate=pl.CostEstimate(flops=2 * 1024 * 4096 * 512, bytes_accessed=1 << 22, transcendentals=0),
        name="segment_sums",
    )(me, table, owner_row.reshape(32, 128), owner_slot.reshape(32, 128), cotangent)

    with jax.named_scope("exchange_grads"):
        got = lax.ppermute(send, "core", SWAP)
        own, one, two, three = pl.pallas_call(
            join_kernel,
            out_shape=(shape((512, EMBED), F32),) + (shape((512, EMBED), BF16),) * 3,
            in_specs=vmem(2),
            out_specs=tuple(vmem(4)),
            compiler_params=params(),
            name="join_cores",
        )(keep, got)
        parts = [lax.ppermute(part, "z", shift(step)) for step, part in ((2, two), (1, one), (3, three))]

    slopes_type = F32
    whole = lambda *dims: pl.BlockSpec(dims, lambda step: (0,) * len(dims))
    by_rows = pl.BlockSpec((256, WIDTH), lambda step: (step, 0))
    by_cols = pl.BlockSpec((512, 256), lambda step: (0, step))
    smem_whole = pl.BlockSpec(memory_space=pltpu.SMEM)
    slope_one, slope_two, enc_t, one_t, two_t = pl.pallas_call(
        forward_kernel,
        grid=(4,),
        out_shape=(shape((WIDTH, WIDTH), slopes_type),) * 2 + (shape((512, WIDTH), BF16),) * 3,
        in_specs=[smem_whole, whole(128, 128), pl.BlockSpec(memory_space=pl.ANY), whole(3, WIDTH),
                  whole(WIDTH, WIDTH), whole(WIDTH, WIDTH)],
        out_specs=(by_rows, by_rows, by_cols, by_cols, by_cols),
        scratch_shapes=[pltpu.VMEM((256, WIDTH), BF16)] * 3,
        compiler_params=params(),
        cost_estimate=pl.CostEstimate(flops=8 * 1024 ** 3, bytes_accessed=1 << 24, transcendentals=1 << 22),
        name="forward",
    )(me, table, one, hash_seeds, w_in, w_mid)

    with jax.named_scope("grad_use"):
        mine = pl.pallas_call(
            total_kernel,
            out_shape=shape((512, EMBED), BF16),
            in_specs=vmem(4) + [pl.BlockSpec(memory_space=pl.ANY)],
            out_specs=vmem(1)[0],
            compiler_params=params(),
            name="total_grads",
        )(own, *parts, two_t)
        other = lax.ppermute(mine, "core", SWAP)

    out = pl.pallas_call(
        backward_kernel,
        grid=(4,),
        out_shape=shape((512, 2176), BF16),
        in_specs=[whole(512, EMBED), whole(512, EMBED), by_rows, by_rows, by_cols, by_cols, by_cols,
                  whole(WIDTH, WIDTH), whole(WIDTH, EMBED)],
        out_specs=whole(512, 2176),
        scratch_shapes=[pltpu.VMEM((512, 2176), F32), pltpu.VMEM((256, WIDTH), BF16),
                        pltpu.VMEM((256, WIDTH), BF16)],
        compiler_params=params(),
        cost_estimate=pl.CostEstimate(flops=9 * 1024 ** 3, bytes_accessed=1 << 24, transcendentals=0),
        name="backward",
    )(mine, other, slope_one, slope_two, enc_t, one_t, two_t, w_mid, w_out)

    with jax.named_scope("sum_devices"):
        pieces = lax.all_to_all(out, ("z", "x", "y"), split_axis=0, concat_axis=0, tiled=True)
        sums = jnp.sum(pieces.reshape(64, 8, 2176).astype(F32), axis=0)
    return sums[:, :1024], sums[:, 1024:2048], sums[:, 2048:]


def solution(mesh):
    fine = Mesh(mesh.devices.reshape(4, 2, 4, 4), ALL)
    split = P(ALL)
    rows = P(ALL, None)
    return jax.shard_map(
        per_device, mesh=fine, in_specs=(rows, split, split, split, split, P(), P(), P(), P()),
        out_specs=(rows, rows, rows), check_vma=False)
```

```python
import jax
import jax.numpy as jnp
from jax import lax
from jax.experimental import pallas as pl
from jax.experimental.pallas import tpu as pltpu
from jax.sharding import Mesh, PartitionSpec as P

PRIME = 65521
HIGH_PRIME = 32749
SLOTS = 1536
LOOKUPS = 4096
WIDTH = 1024
EMBED = 128
ALL = ("z", "core", "x", "y")
VMEM_LIMIT = 24 * 1024 * 1024
ORDER = tuple(z * 16 + x * 4 + y for y in range(4) for z in range(4) for x in range(4))
BF16 = jnp.bfloat16
F32 = jnp.float32
I32 = jnp.int32


def vmem(count):
    return [pl.BlockSpec(memory_space=pltpu.VMEM)] * count


def params(**extra):
    return pltpu.CompilerParams(vmem_limit_bytes=VMEM_LIMIT, **extra)


def owner_ranges(table_ref):
    first = jnp.zeros((1, 1), I32)
    ranges = []
    for owner in range(8):
        count = table_ref[owner * 16 + 12 : owner * 16 + 13, 0:1]
        ranges.append((first, count))
        first = first + count
    return ranges


def segment_kernel(table_ref, row_ref, slot_ref, cot_ref, keep_ref, send_ref, wide, hot):
    z, core = lax.axis_index("z"), lax.axis_index("core")
    owner = row_ref[...]
    place = slot_ref[...]
    for index, (first, _) in enumerate(owner_ranges(table_ref)):
        place = jnp.where(owner == index, place + first, place)
    place = place ^ (core << 9)
    quarter = ((place >> 10) - z) & 3
    inner = place & 1023
    quarter_t = quarter.T
    for chunk in range(32):
        rows = slice(chunk * 128, chunk * 128 + 128)
        column = jnp.broadcast_to(quarter_t[:, chunk : chunk + 1], (128, 128))
        cot = cot_ref[rows, :].astype(F32)
        for part in range(4):
            wide[rows, part * 128 : part * 128 + 128] = jnp.where(column == part, cot, 0.0).astype(BF16)
    for half in (1, 0):
        ids = lax.broadcasted_iota(I32, (512, 128), 0) + half * 512
        for chunk in range(32):
            hit = inner[chunk : chunk + 1, :] == ids
            hot[:, chunk * 128 : chunk * 128 + 128] = jnp.where(hit, 1.0, 0.0).astype(BF16)
        for pair in range(2):
            total = jnp.dot(hot[...], wide[:, pair * 256 : pair * 256 + 256], preferred_element_type=F32)
            for sub in range(2):
                part = pair * 2 + sub
                rows = slice(part * 512, part * 512 + 512)
                piece = total[:, sub * 128 : sub * 128 + 128]
                if half:
                    send_ref[rows, :] = piece.astype(BF16)
                else:
                    keep_ref[rows, :] = piece


def join_kernel(keep_ref, got_ref, after_ref, own_ref, one_ref, two_ref, three_ref):
    own_ref[...] = keep_ref[0:512, :] + got_ref[0:512, :].astype(F32)
    for part, out in enumerate((one_ref, two_ref, three_ref), 1):
        rows = slice(part * 512, part * 512 + 512)
        out[...] = (keep_ref[rows, :] + got_ref[rows, :].astype(F32)).astype(BF16)


def total_kernel(own_ref, one_ref, two_ref, three_ref, after_ref, out_ref):
    total = own_ref[...] + one_ref[...].astype(F32) + two_ref[...].astype(F32) + three_ref[...].astype(F32)
    out_ref[...] = total.astype(BF16)


def mish_parts(value):
    e = jnp.exp(jnp.minimum(value, 20.0))
    n = e * (e + 2.0)
    inverse = 1.0 / (n + 2.0)
    tanh_soft = n * inverse
    twice = inverse + inverse
    return value * tanh_soft, tanh_soft + (value * (n - e)) * (twice * twice)


def pack_kernel(count_ref, ids_ref, out_ref):
    for copy in range(8):
        out_ref[copy, 0:12, :] = ids_ref[...]
        out_ref[copy, 12:16, :] = jnp.full((4, 128), count_ref[0], I32)


def bring_kernel(cot_ref, row_ref, slot_ref, cot_out, row_out, slot_out):
    cot_out[...] = cot_ref[...]
    row_out[...] = row_ref[...]
    slot_out[...] = slot_ref[...]


def prepare_kernel(w_in_ref, w_mid_ref, seeds_ref, after_ref, w_in_t_ref, w_mid_t_ref, seeds_t_ref):
    for part in range(4):
        cols = slice(part * 256, part * 256 + 256)
        w_in_t_ref[cols, :] = w_in_ref[:, cols].T
        w_mid_t_ref[cols, :] = w_mid_ref[:, cols].T
    seeds_t_ref[...] = jnp.concatenate([seeds_ref[...], jnp.zeros((5, WIDTH), I32)], axis=0).T


def find_ids(z, core, table_ref):
    line = lax.broadcasted_iota(I32, (1, WIDTH), 1)
    place = z * 1024 + (line ^ (core << 9))
    where_at = jnp.zeros((1, WIDTH), I32)
    for index, (first, count) in enumerate(owner_ranges(table_ref)):
        inside = (place >= first) & (place < first + count)
        where_at = jnp.where(inside, place - first + index * 2048, where_at)
    sub = lax.broadcasted_iota(I32, (128, WIDTH), 0)
    pick = jnp.where((where_at >> 7) == sub, 1.0, 0.0).astype(BF16)
    table = table_ref[...].T
    found = jnp.zeros((128, WIDTH), F32)
    for shift_by in (0, 8, 16):
        piece = ((table >> shift_by) & 255).astype(F32).astype(BF16)
        found += jnp.dot(piece, pick, preferred_element_type=F32) * float(1 << shift_by)
    return jnp.sum(jnp.where((where_at & 127) == sub, found, 0.0), axis=0, keepdims=True).astype(I32)


def forward_kernel(table_ref, after_ref, seeds_ref, w_in_ref, w_mid_ref,
                   slope_one_ref, slope_two_ref, enc_r_ref, one_r_ref, two_r_ref,
                   codes, enc, one, two):
    z, core = lax.axis_index("z"), lax.axis_index("core")
    ids = find_ids(z, core, table_ref)
    low = (ids >> 16) * 15 + (ids & 65535)
    over = low >= PRIME
    high = (ids >> 16) + jnp.where(over, 1, 0)
    codes[0:1, :] = jnp.where(over, low - PRIME, low)
    codes[1:2, :] = jnp.where(high >= HIGH_PRIME, high - HIGH_PRIME, high)
    for block in range(4):
        cols = slice(block * 256, block * 256 + 256)
        for part in range(4):
            rows = slice(part * 256, part * 256 + 256)
            first, second, offset = (seeds_ref[rows, index : index + 1] for index in range(3))
            mix = first * codes[0:1, cols] + (second * codes[1:2, cols] + offset)
            mix = lax.shift_right_logical(mix, 16) * 15 + (mix & 65535)
            mix = (mix >> 16) * 15 + (mix & 65535)
            mix = jnp.where(mix >= PRIME, mix - PRIME, mix)
            enc[rows, cols] = (mix.astype(F32) * (2.0 / 65520.0) - 1.0).astype(BF16)
        for weights, source, target, slopes in (
            (w_in_ref, enc, one, slope_one_ref), (w_mid_ref, one, two, slope_two_ref)):
            for part in range(4):
                rows = slice(part * 256, part * 256 + 256)
                act, slope = mish_parts(jnp.dot(weights[rows, :], source[:, cols], preferred_element_type=F32))
                target[rows, cols] = act.astype(BF16)
                slopes[rows, cols] = slope
    for part in range(4):
        rows = pl.ds(pl.multiple_of(core * 128 + part * 256, 128), 128)
        out = slice(part * 128, part * 128 + 128)
        enc_r_ref[out, :] = enc[rows, :]
        one_r_ref[out, :] = one[rows, :]
        two_r_ref[out, :] = two[rows, :]


def sum_kernel(pieces_ref, in_ref, mid_ref, last_ref):
    for start, out_ref in ((0, in_ref), (1024, mid_ref), (2048, last_ref)):
        for col in range(0, out_ref.shape[1], 128):
            total = jnp.zeros((16, 128), F32)
            for pair in range(32):
                total += pieces_ref[pair * 16 : pair * 16 + 16, start + col : start + col + 128].astype(F32)
            out_ref[:, col : col + 128] = total[0:8, :] + total[8:16, :]


def in_order(value):
    return jnp.concatenate([value[chip * 8 : chip * 8 + 8, :] for chip in ORDER], axis=0).astype(BF16)


def backward_kernel(mine_ref, other_ref, slope_one_ref, slope_two_ref, enc_ref, one_ref, two_ref,
                    w_mid_ref, w_out_ref, out_ref, delta_two, delta_one):
    nt = (((1,), (1,)), ((), ()))

    tiles = [slice(index * 256, index * 256 + 256) for index in range(4)]
    for rows in tiles:
        for half, grad_ref in enumerate((mine_ref, other_ref)):
            cols = slice(half * 512, half * 512 + 512)
            back = lax.dot_general(w_out_ref[rows, :], grad_ref[...], nt, preferred_element_type=F32)
            delta_two[rows, cols] = (back * slope_two_ref[rows, cols]).astype(BF16)
    for rows in tiles:
        back = jnp.dot(w_mid_ref[rows, :], delta_two[...], preferred_element_type=F32)
        delta_one[rows, :] = (back * slope_one_ref[rows, :]).astype(BF16)
    for index, rows in enumerate(tiles):
        out_ref[:, 1024 + index * 256 : 1280 + index * 256] = in_order(
            lax.dot_general(one_ref[...], delta_two[rows, :], nt, preferred_element_type=F32))
    out_ref[:, 2048:2176] = in_order(
        jnp.dot(two_ref[:, 0:512], mine_ref[...], preferred_element_type=F32)
        + jnp.dot(two_ref[:, 512:1024], other_ref[...], preferred_element_type=F32))
    for rows in tiles:
        out_ref[:, rows] = in_order(
            lax.dot_general(enc_ref[...], delta_one[rows, :], nt, preferred_element_type=F32))


def shift(steps):
    return [(index, (index + steps) % 4) for index in range(4)]


SWAP = [(0, 1), (1, 0)]


def per_device(cotangent, owner_row, owner_slot, counts, unique_ids, hash_seeds, w_in, w_mid, w_out):
    shape = jax.ShapeDtypeStruct

    smem = pl.BlockSpec(memory_space=pltpu.SMEM)
    anywhere = pl.BlockSpec(memory_space=pl.ANY)
    with jax.named_scope("gather_ids"):
        copies = pl.pallas_call(
            pack_kernel,
            out_shape=shape((8, 16, 128), I32),
            in_specs=[smem] + vmem(1),
            out_specs=vmem(1)[0],
            compiler_params=params(),
            name="pack_ids",
        )(counts, unique_ids.reshape(12, 128))
        table = lax.all_to_all(copies, ("z", "core"), split_axis=0, concat_axis=0, tiled=True).reshape(128, 128)
        cot, rows, slots = pl.pallas_call(
            bring_kernel,
            out_shape=(shape((LOOKUPS, EMBED), BF16), shape((32, 128), I32), shape((32, 128), I32)),
            in_specs=vmem(3),
            out_specs=tuple(vmem(3)),
            compiler_params=params(),
            name="bring_lookups",
        )(cotangent, owner_row.reshape(32, 128), owner_slot.reshape(32, 128))

    keep, send = pl.pallas_call(
        segment_kernel,
        out_shape=(shape((2048, EMBED), F32), shape((2048, EMBED), BF16)),
        in_specs=vmem(4),
        out_specs=tuple(vmem(2)),
        scratch_shapes=[pltpu.VMEM((LOOKUPS, 512), BF16), pltpu.VMEM((512, LOOKUPS), BF16)],
        compiler_params=params(),
        cost_estimate=pl.CostEstimate(flops=2 * 1024 * 4096 * 512, bytes_accessed=1 << 22, transcendentals=0),
        name="segment_sums",
    )(table, rows, slots, cot)

    with jax.named_scope("exchange_grads"):
        got = lax.ppermute(send, "core", SWAP)
        w_in_t, w_mid_t, seeds_t = pl.pallas_call(
            prepare_kernel,
            out_shape=(shape((WIDTH, WIDTH), BF16), shape((WIDTH, WIDTH), BF16), shape((WIDTH, 8), I32)),
            in_specs=vmem(3) + [anywhere],
            out_specs=tuple(vmem(3)),
            compiler_params=params(),
            name="transpose_weights",
        )(w_in, w_mid, hash_seeds, send)
        own, one, two, three = pl.pallas_call(
            join_kernel,
            out_shape=(shape((512, EMBED), F32),) + (shape((512, EMBED), BF16),) * 3,
            in_specs=vmem(2) + [anywhere],
            out_specs=tuple(vmem(4)),
            compiler_params=params(),
            name="join_cores",
        )(keep, got, seeds_t)
        parts = [lax.ppermute(part, "z", shift(step)) for step, part in ((2, two), (1, one), (3, three))]

    slope_one, slope_two, enc, one_units, two_units = pl.pallas_call(
        forward_kernel,
        out_shape=(shape((WIDTH, WIDTH), F32),) * 2 + (shape((512, WIDTH), BF16),) * 3,
        in_specs=vmem(1) + [anywhere] + vmem(3),
        out_specs=tuple(vmem(5)),
        scratch_shapes=[pltpu.VMEM((8, WIDTH), I32)] + [pltpu.VMEM((WIDTH, WIDTH), BF16)] * 3,
        compiler_params=params(),
        cost_estimate=pl.CostEstimate(flops=8 * 1024 ** 3, bytes_accessed=1 << 24, transcendentals=1 << 22),
        name="forward",
    )(table, one, seeds_t, w_in_t, w_mid_t)

    with jax.named_scope("grad_use"):
        mine = pl.pallas_call(
            total_kernel,
            out_shape=shape((512, EMBED), BF16),
            in_specs=vmem(4) + [anywhere],
            out_specs=vmem(1)[0],
            compiler_params=params(),
            name="total_grads",
        )(own, *parts, two_units)
        other = lax.ppermute(mine, "core", SWAP)

    out = pl.pallas_call(
        backward_kernel,
        out_shape=shape((512, 2176), BF16),
        in_specs=vmem(9),
        out_specs=vmem(1)[0],
        scratch_shapes=[pltpu.VMEM((WIDTH, WIDTH), BF16)] * 2,
        compiler_params=params(),
        cost_estimate=pl.CostEstimate(flops=9 * 1024 ** 3, bytes_accessed=1 << 24, transcendentals=0),
        name="backward",
    )(mine, other, slope_one, slope_two, enc, one_units, two_units, w_mid, w_out)

    with jax.named_scope("sum_devices"):
        pieces = lax.all_to_all(out, ("y", "z", "x"), split_axis=0, concat_axis=0, tiled=True)
        return pl.pallas_call(
            sum_kernel,
            out_shape=(shape((8, 1024), F32), shape((8, 1024), F32), shape((8, EMBED), F32)),
            in_specs=vmem(1),
            out_specs=tuple(vmem(3)),
            compiler_params=params(),
            name="sum_chips",
        )(pieces)


def solution(mesh):
    fine = Mesh(mesh.devices.reshape(4, 2, 4, 4), ALL)
    split = P(ALL)
    rows = P(ALL, None)
    return jax.shard_map(
        per_device, mesh=fine, in_specs=(rows, split, split, split, split, P(), P(), P(), P()),
        out_specs=(rows, rows, rows), check_vma=False)
```

```python
import jax
import jax.numpy as jnp
from jax import lax
from jax.experimental import pallas as pl
from jax.experimental.pallas import tpu as pltpu
from jax.sharding import Mesh, PartitionSpec as P

PRIME = 65521
HIGH_PRIME = 32749
SLOTS = 1536
LOOKUPS = 4096
WIDTH = 1024
EMBED = 128
SHARE = 512
ALL = ("z", "core", "x", "y")
VMEM_LIMIT = 24 * 1024 * 1024
ORDER = tuple(z * 16 + x * 4 + y for y in range(4) for z in range(4) for x in range(4))
BF16 = jnp.bfloat16
F32 = jnp.float32
I32 = jnp.int32


def vmem(count):
    return [pl.BlockSpec(memory_space=pltpu.VMEM)] * count


def params(limit=VMEM_LIMIT):
    return pltpu.CompilerParams(vmem_limit_bytes=limit)


def owner_ranges(table_ref):
    first = jnp.zeros((1, 1), I32)
    ranges = []
    for owner in range(8):
        count = table_ref[owner * 16 + 12 : owner * 16 + 13, 0:1]
        ranges.append((first, count))
        first = first + count
    return ranges


def segment_kernel(table_ref, row_ref, slot_ref, cot_ref, keep_ref, send_ref, wide, hot):
    z, core = lax.axis_index("z"), lax.axis_index("core")
    owner = row_ref[...]
    place = slot_ref[...]
    for index, (first, _) in enumerate(owner_ranges(table_ref)):
        place = jnp.where(owner == index, place + first, place)
    place = place ^ (core << 9)
    quarter = ((place >> 10) - z) & 3
    inner = place & 1023
    quarter_t = quarter.T
    ids = lax.broadcasted_iota(I32, (1024, 128), 0)
    for chunk in range(32):
        rows = slice(chunk * 128, chunk * 128 + 128)
        column = jnp.broadcast_to(quarter_t[:, chunk : chunk + 1], (128, 128))
        cot = cot_ref[rows, :].astype(F32)
        for part in range(4):
            wide[rows, part * 128 : part * 128 + 128] = jnp.where(column == part, cot, 0.0).astype(BF16)
        hot[:, rows] = jnp.where(inner[chunk : chunk + 1, :] == ids, 1.0, 0.0).astype(BF16)
    for pair in range(2):
        total = jnp.dot(hot[...], wide[:, pair * 256 : pair * 256 + 256], preferred_element_type=F32)
        for sub in range(2):
            part = pair * 2 + sub
            rows = slice(part * 512, part * 512 + 512)
            cols = slice(sub * 128, sub * 128 + 128)
            keep_ref[rows, :] = total[0:512, cols]
            send_ref[rows, :] = total[512:1024, cols].astype(BF16)


def join_kernel(keep_ref, got_ref, after_ref, own_ref, one_ref, two_ref, three_ref):
    own_ref[...] = keep_ref[0:512, :] + got_ref[0:512, :].astype(F32)
    for part, out in enumerate((one_ref, two_ref, three_ref), 1):
        rows = slice(part * 512, part * 512 + 512)
        out[...] = (keep_ref[rows, :] + got_ref[rows, :].astype(F32)).astype(BF16)


def total_kernel(own_ref, one_ref, two_ref, three_ref, after_ref, out_ref):
    total = own_ref[...] + one_ref[...].astype(F32) + two_ref[...].astype(F32) + three_ref[...].astype(F32)
    out_ref[...] = total.astype(BF16)


def mish_parts(value):
    e = jnp.exp(jnp.minimum(value, 20.0))
    n = e * (e + 2.0)
    inverse = 1.0 / (n + 2.0)
    tanh_soft = n * inverse
    twice = inverse + inverse
    return value * tanh_soft, tanh_soft + (value * (n - e)) * (twice * twice)


def pack_kernel(count_ref, ids_ref, out_ref):
    for copy in range(8):
        out_ref[copy, 0:12, :] = ids_ref[...]
        out_ref[copy, 12:16, :] = jnp.full((4, 128), count_ref[0], I32)


def bring_kernel(cot_ref, row_ref, slot_ref, cot_out, row_out, slot_out):
    cot_out[...] = cot_ref[...]
    row_out[...] = row_ref[...]
    slot_out[...] = slot_ref[...]


def prepare_kernel(w_in_ref, w_mid_ref, seeds_ref, after_ref, w_in_t_ref, w_mid_t_ref, seeds_t_ref):
    for part in range(4):
        cols = slice(part * 256, part * 256 + 256)
        w_in_t_ref[cols, :] = w_in_ref[:, cols].T
        w_mid_t_ref[cols, :] = w_mid_ref[:, cols].T
    seeds_t_ref[...] = jnp.concatenate([seeds_ref[...], jnp.zeros((5, WIDTH), I32)], axis=0).T


def find_ids(z, core, table_ref):
    place = lax.broadcasted_iota(I32, (1, SHARE), 1) + (z * 2 + core) * SHARE
    where_at = jnp.zeros((1, SHARE), I32)
    for index, (first, count) in enumerate(owner_ranges(table_ref)):
        inside = (place >= first) & (place < first + count)
        where_at = jnp.where(inside, place - first + index * 2048, where_at)
    sub = lax.broadcasted_iota(I32, (128, SHARE), 0)
    pick = jnp.where((where_at >> 7) == sub, 1.0, 0.0).astype(BF16)
    table = table_ref[...].T
    found = jnp.zeros((128, SHARE), F32)
    for shift_by in (0, 8, 16):
        piece = ((table >> shift_by) & 255).astype(F32).astype(BF16)
        found += jnp.dot(piece, pick, preferred_element_type=F32) * float(1 << shift_by)
    return jnp.sum(jnp.where((where_at & 127) == sub, found, 0.0), axis=0, keepdims=True).astype(I32)


def forward_kernel(table_ref, after_ref, seeds_ref, w_in_ref, w_mid_ref,
                   slope_one_ref, slope_two_ref, enc_r_ref, one_r_ref, two_r_ref,
                   codes, enc, one, two):
    z, core = lax.axis_index("z"), lax.axis_index("core")
    ids = find_ids(z, core, table_ref)
    low = (ids >> 16) * 15 + (ids & 65535)
    over = low >= PRIME
    high = (ids >> 16) + jnp.where(over, 1, 0)
    codes[0:1, :] = jnp.where(over, low - PRIME, low)
    codes[1:2, :] = jnp.where(high >= HIGH_PRIME, high - HIGH_PRIME, high)
    for block in range(2):
        cols = slice(block * 256, block * 256 + 256)
        for part in range(4):
            rows = slice(part * 256, part * 256 + 256)
            first, second, offset = (seeds_ref[rows, index : index + 1] for index in range(3))
            mix = first * codes[0:1, cols] + (second * codes[1:2, cols] + offset)
            mix = lax.shift_right_logical(mix, 16) * 15 + (mix & 65535)
            mix = (mix >> 16) * 15 + (mix & 65535)
            mix = jnp.where(mix >= PRIME, mix - PRIME, mix)
            enc[rows, cols] = (mix.astype(F32) * (2.0 / 65520.0) - 1.0).astype(BF16)
        for weights, source, target, slopes in (
            (w_in_ref, enc, one, slope_one_ref), (w_mid_ref, one, two, slope_two_ref)):
            for part in range(4):
                rows = slice(part * 256, part * 256 + 256)
                act, slope = mish_parts(jnp.dot(weights[rows, :], source[:, cols], preferred_element_type=F32))
                target[rows, cols] = act.astype(BF16)
                slopes[rows, cols] = slope
    for half in range(2):
        for part in range(4):
            rows = pl.ds(pl.multiple_of((core ^ half) * 128 + part * 256, 128), 128)
            out = slice(half * 512 + part * 128, half * 512 + part * 128 + 128)
            enc_r_ref[out, :] = enc[rows, :]
            one_r_ref[out, :] = one[rows, :]
            two_r_ref[out, :] = two[rows, :]


def sum_kernel(pieces_ref, in_ref, mid_ref, last_ref):
    for start, out_ref in ((0, in_ref), (1024, mid_ref), (2048, last_ref)):
        for col in range(0, out_ref.shape[1], 128):
            total = jnp.zeros((16, 128), F32)
            for pair in range(32):
                total += pieces_ref[pair * 16 : pair * 16 + 16, start + col : start + col + 128].astype(F32)
            out_ref[:, col : col + 128] = total[0:8, :] + total[8:16, :]


def in_order(value):
    return jnp.concatenate([value[chip * 8 : chip * 8 + 8, :] for chip in ORDER], axis=0).astype(BF16)


NT = (((1,), (1,)), ((), ()))
TILES = tuple(slice(index * 256, index * 256 + 256) for index in range(4))


def backward_two_kernel(grad_ref, slope_ref, one_ref, two_ref, w_out_ref, delta_ref, own_ref, send_ref):
    for rows in TILES:
        back = lax.dot_general(w_out_ref[rows, :], grad_ref[...], NT, preferred_element_type=F32)
        delta_ref[rows, :] = (back * slope_ref[rows, :]).astype(BF16)
    for cols in TILES:
        total = lax.dot_general(one_ref[...], delta_ref[cols, :], NT, preferred_element_type=F32)
        own_ref[:, cols] = total[0:512, :]
        send_ref[:, cols] = total[512:1024, :].astype(BF16)
    total = jnp.dot(two_ref[...], grad_ref[...], preferred_element_type=F32)
    own_ref[:, 1024:1152] = total[0:512, :]
    send_ref[:, 1024:1152] = total[512:1024, :].astype(BF16)


def backward_one_kernel(delta_two_ref, slope_ref, enc_ref, w_mid_ref, own_ref, send_ref, delta):
    for rows in TILES:
        back = jnp.dot(w_mid_ref[rows, :], delta_two_ref[...], preferred_element_type=F32)
        delta[rows, :] = (back * slope_ref[rows, :]).astype(BF16)
    for cols in TILES:
        total = lax.dot_general(enc_ref[...], delta[cols, :], NT, preferred_element_type=F32)
        own_ref[:, cols] = total[0:512, :]
        send_ref[:, cols] = total[512:1024, :].astype(BF16)


def merge_kernel(own_one_ref, got_one_ref, own_two_ref, got_two_ref, out_ref):
    for start, own_ref, got_ref in ((0, own_one_ref, got_one_ref), (1024, own_two_ref, got_two_ref)):
        for col in range(0, own_ref.shape[1], 128):
            cols = slice(col, col + 128)
            out_ref[:, start + col : start + col + 128] = in_order(own_ref[:, cols] + got_ref[:, cols].astype(F32))


def shift(steps):
    return [(index, (index + steps) % 4) for index in range(4)]


SWAP = [(0, 1), (1, 0)]


def per_device(cotangent, owner_row, owner_slot, counts, unique_ids, hash_seeds, w_in, w_mid, w_out):
    shape = jax.ShapeDtypeStruct

    smem = pl.BlockSpec(memory_space=pltpu.SMEM)
    anywhere = pl.BlockSpec(memory_space=pl.ANY)
    with jax.named_scope("gather_ids"):
        copies = pl.pallas_call(
            pack_kernel,
            out_shape=shape((8, 16, 128), I32),
            in_specs=[smem] + vmem(1),
            out_specs=vmem(1)[0],
            compiler_params=params(60 * 1024 * 1024),
            name="pack_ids",
        )(counts, unique_ids.reshape(12, 128))
        table = lax.all_to_all(copies, ("z", "core"), split_axis=0, concat_axis=0, tiled=True).reshape(128, 128)
        cot, rows, slots = pl.pallas_call(
            bring_kernel,
            out_shape=(shape((LOOKUPS, EMBED), BF16), shape((32, 128), I32), shape((32, 128), I32)),
            in_specs=vmem(3),
            out_specs=tuple(vmem(3)),
            compiler_params=params(),
            name="bring_lookups",
        )(cotangent, owner_row.reshape(32, 128), owner_slot.reshape(32, 128))

    keep, send = pl.pallas_call(
        segment_kernel,
        out_shape=(shape((2048, EMBED), F32), shape((2048, EMBED), BF16)),
        in_specs=vmem(4),
        out_specs=tuple(vmem(2)),
        scratch_shapes=[pltpu.VMEM((LOOKUPS, 512), BF16), pltpu.VMEM((1024, LOOKUPS), BF16)],
        compiler_params=params(),
        cost_estimate=pl.CostEstimate(flops=2 * 1024 * 4096 * 512, bytes_accessed=1 << 22, transcendentals=0),
        name="segment_sums",
    )(table, rows, slots, cot)

    with jax.named_scope("exchange_grads"):
        got = lax.ppermute(send, "core", SWAP)
        w_in_t, w_mid_t, seeds_t = pl.pallas_call(
            prepare_kernel,
            out_shape=(shape((WIDTH, WIDTH), BF16), shape((WIDTH, WIDTH), BF16), shape((WIDTH, 8), I32)),
            in_specs=vmem(3) + [anywhere],
            out_specs=tuple(vmem(3)),
            compiler_params=params(),
            name="transpose_weights",
        )(w_in, w_mid, hash_seeds, send)
        own, one, two, three = pl.pallas_call(
            join_kernel,
            out_shape=(shape((512, EMBED), F32),) + (shape((512, EMBED), BF16),) * 3,
            in_specs=vmem(2) + [anywhere],
            out_specs=tuple(vmem(4)),
            compiler_params=params(),
            name="join_cores",
        )(keep, got, seeds_t)
        parts = [lax.ppermute(part, "z", shift(step)) for step, part in ((2, two), (1, one), (3, three))]

    slope_one, slope_two, enc, one_units, two_units = pl.pallas_call(
        forward_kernel,
        out_shape=(shape((WIDTH, SHARE), F32),) * 2 + (shape((WIDTH, SHARE), BF16),) * 3,
        in_specs=vmem(1) + [anywhere] + vmem(3),
        out_specs=tuple(vmem(5)),
        scratch_shapes=[pltpu.VMEM((8, SHARE), I32)] + [pltpu.VMEM((WIDTH, SHARE), BF16)] * 3,
        compiler_params=params(),
        cost_estimate=pl.CostEstimate(flops=4 * 1024 ** 3, bytes_accessed=1 << 24, transcendentals=1 << 21),
        name="forward",
    )(table, one, seeds_t, w_in_t, w_mid_t)

    with jax.named_scope("grad_use"):
        grads = pl.pallas_call(
            total_kernel,
            out_shape=shape((SHARE, EMBED), BF16),
            in_specs=vmem(4) + [anywhere],
            out_specs=vmem(1)[0],
            compiler_params=params(),
            name="total_grads",
        )(own, *parts, two_units)

    with jax.named_scope("backward"):
        delta_two, own_two, send_two = pl.pallas_call(
            backward_two_kernel,
            out_shape=(shape((WIDTH, SHARE), BF16), shape((512, 1152), F32), shape((512, 1152), BF16)),
            in_specs=vmem(5),
            out_specs=tuple(vmem(3)),
            compiler_params=params(),
            name="backward_two",
        )(grads, slope_two, one_units, two_units, w_out)
        got_two = lax.ppermute(send_two, "core", SWAP)
        own_one, send_one = pl.pallas_call(
            backward_one_kernel,
            out_shape=(shape((512, 1024), F32), shape((512, 1024), BF16)),
            in_specs=vmem(4),
            out_specs=tuple(vmem(2)),
            scratch_shapes=[pltpu.VMEM((WIDTH, SHARE), BF16)],
            compiler_params=params(),
            name="backward_one",
        )(delta_two, slope_one, enc, w_mid)
        got_one = lax.ppermute(send_one, "core", SWAP)
        out = pl.pallas_call(
            merge_kernel,
            out_shape=shape((512, 2176), BF16),
            in_specs=vmem(4),
            out_specs=vmem(1)[0],
            compiler_params=params(),
            name="merge_cores",
        )(own_one, got_one, own_two, got_two)

    with jax.named_scope("sum_devices"):
        pieces = lax.all_to_all(out, ("y", "z", "x"), split_axis=0, concat_axis=0, tiled=True)
        return pl.pallas_call(
            sum_kernel,
            out_shape=(shape((8, 1024), F32), shape((8, 1024), F32), shape((8, EMBED), F32)),
            in_specs=vmem(1),
            out_specs=tuple(vmem(3)),
            compiler_params=params(),
            name="sum_chips",
        )(pieces)


def solution(mesh):
    fine = Mesh(mesh.devices.reshape(4, 2, 4, 4), ALL)
    split = P(ALL)
    rows = P(ALL, None)
    return jax.shard_map(
        per_device, mesh=fine, in_specs=(rows, split, split, split, split, P(), P(), P(), P()),
        out_specs=(rows, rows, rows), check_vma=False)
```

```python
import jax
import jax.numpy as jnp
from jax import lax
from jax.experimental import pallas as pl
from jax.experimental.pallas import tpu as pltpu
from jax.sharding import Mesh, PartitionSpec as P

PRIME = 65521
HIGH_PRIME = 32749
SLOTS = 1536
LOOKUPS = 4096
WIDTH = 1024
EMBED = 128
SHARE = 512
ALL = ("z", "core", "x", "y")
VMEM_LIMIT = 24 * 1024 * 1024
PACK_LIMIT = 24 * 1024 * 1024
BY_COLUMN = tuple(z * 16 + column for column in range(16) for z in range(4))
BF16 = jnp.bfloat16
F32 = jnp.float32
I32 = jnp.int32


def vmem(count):
    return [pl.BlockSpec(memory_space=pltpu.VMEM)] * count


def params(limit=VMEM_LIMIT):
    return pltpu.CompilerParams(vmem_limit_bytes=limit)


def owner_ranges(table_ref):
    first = jnp.zeros((1, 1), I32)
    ranges = []
    for owner in range(8):
        count = table_ref[owner * 16 + 12 : owner * 16 + 13, 0:1]
        ranges.append((first, count))
        first = first + count
    return ranges


def segment_kernel(table_ref, row_ref, slot_ref, cot_ref, keep_ref, send_ref, wide, hot):
    z, core = lax.axis_index("z"), lax.axis_index("core")
    owner = row_ref[...]
    place = slot_ref[...]
    for index, (first, _) in enumerate(owner_ranges(table_ref)):
        place = jnp.where(owner == index, place + first, place)
    place = place ^ (core << 9)
    quarter = ((place >> 10) - z) & 3
    inner = place & 1023
    quarter_t = quarter.T
    ids = lax.broadcasted_iota(I32, (1024, 128), 0)
    for chunk in range(32):
        rows = slice(chunk * 128, chunk * 128 + 128)
        column = jnp.broadcast_to(quarter_t[:, chunk : chunk + 1], (128, 128))
        cot = cot_ref[rows, :].astype(F32)
        for part in range(4):
            wide[rows, part * 128 : part * 128 + 128] = jnp.where(column == part, cot, 0.0).astype(BF16)
        hot[:, rows] = jnp.where(inner[chunk : chunk + 1, :] == ids, 1.0, 0.0).astype(BF16)
    for pair in range(2):
        total = jnp.dot(hot[...], wide[:, pair * 256 : pair * 256 + 256], preferred_element_type=F32)
        for sub in range(2):
            part = pair * 2 + sub
            rows = slice(part * 512, part * 512 + 512)
            cols = slice(sub * 128, sub * 128 + 128)
            keep_ref[rows, :] = total[0:512, cols]
            send_ref[rows, :] = total[512:1024, cols].astype(BF16)


def join_kernel(keep_ref, got_ref, after_ref, own_ref, one_ref, two_ref, three_ref):
    own_ref[...] = keep_ref[0:512, :] + got_ref[0:512, :].astype(F32)
    for part, out in enumerate((one_ref, two_ref, three_ref), 1):
        rows = slice(part * 512, part * 512 + 512)
        out[...] = (keep_ref[rows, :] + got_ref[rows, :].astype(F32)).astype(BF16)


def total_kernel(own_ref, one_ref, two_ref, three_ref, after_ref, out_ref):
    total = own_ref[...] + one_ref[...].astype(F32) + two_ref[...].astype(F32) + three_ref[...].astype(F32)
    out_ref[...] = total.astype(BF16)


def mish_parts(value):
    e = jnp.exp(jnp.minimum(value, 20.0))
    n = e * (e + 2.0)
    inverse = 1.0 / (n + 2.0)
    tanh_soft = n * inverse
    twice = inverse + inverse
    return value * tanh_soft, tanh_soft + (value * (n - e)) * (twice * twice)


def pack_kernel(count_ref, ids_ref, cot_ref, row_ref, slot_ref,
                out_ref, cot_out, row_out, slot_out, ids, sems):
    pairs = ((ids_ref, ids), (cot_ref, cot_out), (row_ref, row_out), (slot_ref, slot_out))
    copies = [pltpu.make_async_copy(source, target, sems.at[index]) for index, (source, target) in enumerate(pairs)]
    for copy in copies:
        copy.start()
    copies[0].wait()
    for copy in range(8):
        out_ref[copy, 0:12, :] = ids[...]
        out_ref[copy, 12:16, :] = jnp.full((4, 128), count_ref[0], I32)
    for copy in copies[1:]:
        copy.wait()


def prepare_kernel(w_in_ref, w_mid_ref, seeds_ref, after_ref, w_in_t_ref, w_mid_t_ref, seeds_t_ref):
    for part in range(4):
        cols = slice(part * 256, part * 256 + 256)
        w_in_t_ref[cols, :] = w_in_ref[:, cols].T
        w_mid_t_ref[cols, :] = w_mid_ref[:, cols].T
    seeds_t_ref[...] = jnp.concatenate([seeds_ref[...], jnp.zeros((5, WIDTH), I32)], axis=0).T


def find_ids(z, core, table_ref):
    place = lax.broadcasted_iota(I32, (1, SHARE), 1) + (z * 2 + core) * SHARE
    where_at = jnp.zeros((1, SHARE), I32)
    for index, (first, count) in enumerate(owner_ranges(table_ref)):
        inside = (place >= first) & (place < first + count)
        where_at = jnp.where(inside, place - first + index * 2048, where_at)
    sub = lax.broadcasted_iota(I32, (128, SHARE), 0)
    pick = jnp.where((where_at >> 7) == sub, 1.0, 0.0).astype(BF16)
    table = table_ref[...].T
    found = jnp.zeros((128, SHARE), F32)
    for shift_by in (0, 8, 16):
        piece = ((table >> shift_by) & 255).astype(F32).astype(BF16)
        found += jnp.dot(piece, pick, preferred_element_type=F32) * float(1 << shift_by)
    return jnp.sum(jnp.where((where_at & 127) == sub, found, 0.0), axis=0, keepdims=True).astype(I32)


def forward_kernel(table_ref, after_ref, seeds_ref, w_in_ref, w_mid_ref,
                   slope_one_ref, slope_two_ref, enc_r_ref, one_r_ref, two_r_ref,
                   codes, enc, one, two):
    z, core = lax.axis_index("z"), lax.axis_index("core")
    ids = find_ids(z, core, table_ref)
    low = (ids >> 16) * 15 + (ids & 65535)
    over = low >= PRIME
    high = (ids >> 16) + jnp.where(over, 1, 0)
    codes[0:1, :] = jnp.where(over, low - PRIME, low)
    codes[1:2, :] = jnp.where(high >= HIGH_PRIME, high - HIGH_PRIME, high)
    for block in range(2):
        cols = slice(block * 256, block * 256 + 256)
        for part in range(4):
            rows = slice(part * 256, part * 256 + 256)
            first, second, offset = (seeds_ref[rows, index : index + 1] for index in range(3))
            mix = first * codes[0:1, cols] + (second * codes[1:2, cols] + offset)
            mix = lax.shift_right_logical(mix, 16) * 15 + (mix & 65535)
            mix = (mix >> 16) * 15 + (mix & 65535)
            mix = jnp.where(mix >= PRIME, mix - PRIME, mix)
            enc[rows, cols] = (mix.astype(F32) * (2.0 / 65520.0) - 1.0).astype(BF16)
        for weights, source, target, slopes in (
            (w_in_ref, enc, one, slope_one_ref), (w_mid_ref, one, two, slope_two_ref)):
            for part in range(4):
                rows = slice(part * 256, part * 256 + 256)
                act, slope = mish_parts(jnp.dot(weights[rows, :], source[:, cols], preferred_element_type=F32))
                target[rows, cols] = act.astype(BF16)
                slopes[rows, cols] = slope
    for half in range(2):
        for part in range(4):
            rows = pl.ds(pl.multiple_of((core ^ half) * 128 + part * 256, 128), 128)
            out = slice(half * 512 + part * 128, half * 512 + part * 128 + 128)
            enc_r_ref[out, :] = enc[rows, :]
            one_r_ref[out, :] = one[rows, :]
            two_r_ref[out, :] = two[rows, :]


NT = (((1,), (1,)), ((), ()))
TILES = tuple(slice(index * 256, index * 256 + 256) for index in range(4))


def backward_two_kernel(grad_ref, slope_ref, one_ref, two_ref, w_out_ref, delta_ref, own_ref, send_ref):
    for rows in TILES:
        back = lax.dot_general(w_out_ref[rows, :], grad_ref[...], NT, preferred_element_type=F32)
        delta_ref[rows, :] = (back * slope_ref[rows, :]).astype(BF16)
    for cols in TILES:
        total = lax.dot_general(one_ref[...], delta_ref[cols, :], NT, preferred_element_type=F32)
        own_ref[:, cols] = total[0:512, :]
        send_ref[:, cols] = total[512:1024, :].astype(BF16)
    total = jnp.dot(two_ref[...], grad_ref[...], preferred_element_type=F32)
    own_ref[:, 1024:1152] = total[0:512, :]
    send_ref[:, 1024:1152] = total[512:1024, :].astype(BF16)


def backward_one_kernel(delta_two_ref, slope_ref, enc_ref, w_mid_ref, own_ref, send_ref, delta):
    for rows in TILES:
        back = jnp.dot(w_mid_ref[rows, :], delta_two_ref[...], preferred_element_type=F32)
        delta[rows, :] = (back * slope_ref[rows, :]).astype(BF16)
    for cols in TILES:
        total = lax.dot_general(enc_ref[...], delta[cols, :], NT, preferred_element_type=F32)
        own_ref[:, cols] = total[0:512, :]
        send_ref[:, cols] = total[512:1024, :].astype(BF16)


def merge_two_kernel(own_ref, got_ref, keep_ref, one_ref, two_ref, three_ref):
    z = lax.axis_index("z")
    for step, out_ref in enumerate((keep_ref, one_ref, two_ref, three_ref)):
        rows = pl.ds(pl.multiple_of(((z + step) & 3) * 128, 128), 128)
        out_ref[...] = (own_ref[rows, :] + got_ref[rows, :].astype(F32)).astype(out_ref.dtype)


def merge_one_kernel(own_ref, got_ref, after_ref, out_ref):
    for col in range(0, 1024, 128):
        cols = slice(col, col + 128)
        value = own_ref[:, cols] + got_ref[:, cols].astype(F32)
        out_ref[:, cols] = jnp.concatenate(
            [value[chip * 8 : chip * 8 + 8, :] for chip in BY_COLUMN], axis=0).astype(BF16)


def sum_columns_kernel(pieces_ref, keep_ref, one_ref, two_ref, three_ref, total):
    z = lax.axis_index("z")
    for col in range(0, 1024, 128):
        cols = slice(col, col + 128)
        total[:, cols] = sum(pieces_ref[piece * 32 : piece * 32 + 32, cols].astype(F32) for piece in range(16))
    for step, out_ref in enumerate((keep_ref, one_ref, two_ref, three_ref)):
        out_ref[...] = total[pl.ds(pl.multiple_of(((z + step) & 3) * 8, 8), 8), :]


def sum_rows_kernel(keep_ref, one_ref, two_ref, three_ref, after_ref, out_ref):
    total = keep_ref[...] + one_ref[...].astype(F32) + two_ref[...].astype(F32) + three_ref[...].astype(F32)
    out_ref[...] = total.astype(BF16)


def last_kernel(keep_ref, one_ref, two_ref, three_ref, pieces_ref, in_ref, mid_ref, last_ref):
    in_ref[...] = (keep_ref[...] + one_ref[...]) + (two_ref[...] + three_ref[...])
    for start, out_ref in ((0, mid_ref), (1024, last_ref)):
        for col in range(0, out_ref.shape[1], 128):
            cols = slice(start + col, start + col + 128)
            total = sum(pieces_ref[piece * 16 : piece * 16 + 16, cols].astype(F32) for piece in range(8))
            out_ref[:, col : col + 128] = total[0:8, :] + total[8:16, :]


def shift(steps):
    return [(index, (index + steps) % 4) for index in range(4)]


SWAP = [(0, 1), (1, 0)]


def per_device(cotangent, owner_row, owner_slot, counts, unique_ids, hash_seeds, w_in, w_mid, w_out):
    shape = jax.ShapeDtypeStruct

    anywhere = pl.BlockSpec(memory_space=pl.ANY)
    with jax.named_scope("gather_ids"):
        copies, cot, rows, slots = pl.pallas_call(
            pack_kernel,
            out_shape=(shape((8, 16, 128), I32), shape((LOOKUPS, EMBED), BF16),
                       shape((32, 128), I32), shape((32, 128), I32)),
            in_specs=[pl.BlockSpec(memory_space=pltpu.SMEM)] + [pl.BlockSpec(memory_space=pltpu.HBM)] * 4,
            out_specs=tuple(vmem(4)),
            scratch_shapes=[pltpu.VMEM((12, 128), I32), pltpu.SemaphoreType.DMA((4,))],
            compiler_params=params(PACK_LIMIT),
            name="pack_ids",
        )(counts, *(pltpu.with_memory_space_constraint(value, pltpu.HBM) for value in (
            unique_ids.reshape(12, 128), cotangent, owner_row.reshape(32, 128), owner_slot.reshape(32, 128))))
        table = lax.all_to_all(copies, ("z", "core"), split_axis=0, concat_axis=0, tiled=True).reshape(128, 128)

    keep, send = pl.pallas_call(
        segment_kernel,
        out_shape=(shape((2048, EMBED), F32), shape((2048, EMBED), BF16)),
        in_specs=vmem(4),
        out_specs=tuple(vmem(2)),
        scratch_shapes=[pltpu.VMEM((LOOKUPS, 512), BF16), pltpu.VMEM((1024, LOOKUPS), BF16)],
        compiler_params=params(),
        cost_estimate=pl.CostEstimate(flops=2 * 1024 * 4096 * 512, bytes_accessed=1 << 22, transcendentals=0),
        name="segment_sums",
    )(table, rows, slots, cot)

    with jax.named_scope("exchange_grads"):
        got = lax.ppermute(send, "core", SWAP)
        w_in_t, w_mid_t, seeds_t = pl.pallas_call(
            prepare_kernel,
            out_shape=(shape((WIDTH, WIDTH), BF16), shape((WIDTH, WIDTH), BF16), shape((WIDTH, 8), I32)),
            in_specs=vmem(3) + [anywhere],
            out_specs=tuple(vmem(3)),
            compiler_params=params(),
            name="transpose_weights",
        )(w_in, w_mid, hash_seeds, send)
        own, one, two, three = pl.pallas_call(
            join_kernel,
            out_shape=(shape((512, EMBED), F32),) + (shape((512, EMBED), BF16),) * 3,
            in_specs=vmem(2) + [anywhere],
            out_specs=tuple(vmem(4)),
            compiler_params=params(),
            name="join_cores",
        )(keep, got, seeds_t)
        parts = [lax.ppermute(part, "z", shift(step)) for step, part in ((2, two), (1, one), (3, three))]

    slope_one, slope_two, enc, one_units, two_units = pl.pallas_call(
        forward_kernel,
        out_shape=(shape((WIDTH, SHARE), F32),) * 2 + (shape((WIDTH, SHARE), BF16),) * 3,
        in_specs=vmem(1) + [anywhere] + vmem(3),
        out_specs=tuple(vmem(5)),
        scratch_shapes=[pltpu.VMEM((8, SHARE), I32)] + [pltpu.VMEM((WIDTH, SHARE), BF16)] * 3,
        compiler_params=params(),
        cost_estimate=pl.CostEstimate(flops=4 * 1024 ** 3, bytes_accessed=1 << 24, transcendentals=1 << 21),
        name="forward",
    )(table, one, seeds_t, w_in_t, w_mid_t)

    with jax.named_scope("grad_use"):
        grads = pl.pallas_call(
            total_kernel,
            out_shape=shape((SHARE, EMBED), BF16),
            in_specs=vmem(4) + [anywhere],
            out_specs=vmem(1)[0],
            compiler_params=params(),
            name="total_grads",
        )(own, *parts, two_units)

    with jax.named_scope("backward"):
        delta_two, own_two, send_two = pl.pallas_call(
            backward_two_kernel,
            out_shape=(shape((WIDTH, SHARE), BF16), shape((512, 1152), F32), shape((512, 1152), BF16)),
            in_specs=vmem(5),
            out_specs=tuple(vmem(3)),
            compiler_params=params(),
            name="backward_two",
        )(grads, slope_two, one_units, two_units, w_out)
        got_two = lax.ppermute(send_two, "core", SWAP)
        own_one, send_one = pl.pallas_call(
            backward_one_kernel,
            out_shape=(shape((512, 1024), F32), shape((512, 1024), BF16)),
            in_specs=vmem(4),
            out_specs=tuple(vmem(2)),
            scratch_shapes=[pltpu.VMEM((WIDTH, SHARE), BF16)],
            compiler_params=params(),
            name="backward_one",
        )(delta_two, slope_one, enc, w_mid)
        got_one = lax.ppermute(send_one, "core", SWAP)

    with jax.named_scope("sum_devices"):
        keep_two, *pieces = pl.pallas_call(
            merge_two_kernel,
            out_shape=(shape((128, 1152), F32),) + (shape((128, 1152), BF16),) * 3,
            in_specs=vmem(2),
            out_specs=tuple(vmem(4)),
            compiler_params=params(),
            name="merge_two",
        )(own_two, got_two)
        rows_two = [lax.ppermute(pieces[step - 1], "z", shift(step)) for step in (2, 1, 3)]
        out_one = pl.pallas_call(
            merge_one_kernel,
            out_shape=shape((512, 1024), BF16),
            in_specs=vmem(2) + [anywhere],
            out_specs=vmem(1)[0],
            compiler_params=params(),
            name="merge_one",
        )(own_one, got_one, pieces[0])
        columns_one = lax.all_to_all(out_one, ("x", "y"), split_axis=0, concat_axis=0, tiled=True)
        keep_one, *pieces = pl.pallas_call(
            sum_columns_kernel,
            out_shape=(shape((8, 1024), F32),) * 4,
            in_specs=vmem(1),
            out_specs=tuple(vmem(4)),
            scratch_shapes=[pltpu.VMEM((32, 1024), F32)],
            compiler_params=params(),
            name="sum_columns",
        )(columns_one)
        rows_one = [lax.ppermute(pieces[step - 1], "z", shift(step)) for step in (2, 1, 3)]
        out_two = pl.pallas_call(
            sum_rows_kernel,
            out_shape=shape((128, 1152), BF16),
            in_specs=vmem(4) + [anywhere],
            out_specs=vmem(1)[0],
            compiler_params=params(),
            name="sum_rows",
        )(keep_two, *rows_two, pieces[0])
        columns_two = lax.all_to_all(out_two, ("x", "y"), split_axis=0, concat_axis=0, tiled=True)
        return pl.pallas_call(
            last_kernel,
            out_shape=(shape((8, 1024), F32), shape((8, 1024), F32), shape((8, EMBED), F32)),
            in_specs=vmem(5),
            out_specs=tuple(vmem(3)),
            compiler_params=params(),
            name="last_sums",
        )(keep_one, *rows_one, columns_two)


def solution(mesh):
    fine = Mesh(mesh.devices.reshape(4, 2, 4, 4), ALL)
    split = P(ALL)
    rows = P(ALL, None)
    return jax.shard_map(
        per_device, mesh=fine, in_specs=(rows, split, split, split, split, P(), P(), P(), P()),
        out_specs=(rows, rows, rows), check_vma=False)
```

```python
import jax
import jax.numpy as jnp
from jax import lax
from jax.experimental import pallas as pl
from jax.experimental.pallas import tpu as pltpu
from jax.sharding import Mesh, PartitionSpec as P

PRIME = 65521
HIGH_PRIME = 32749
SLOTS = 1536
LOOKUPS = 4096
WIDTH = 1024
EMBED = 128
SHARE = 512
ALL = ("z", "core", "x", "y")
VMEM_LIMIT = 24 * 1024 * 1024
PACK_LIMIT = 24 * 1024 * 1024
BY_COLUMN = tuple(z * 16 + column for column in range(16) for z in range(4))
BF16 = jnp.bfloat16
F32 = jnp.float32
I32 = jnp.int32


def vmem(count):
    return [pl.BlockSpec(memory_space=pltpu.VMEM)] * count


def params(limit=VMEM_LIMIT):
    return pltpu.CompilerParams(vmem_limit_bytes=limit)


def owner_ranges(table_ref):
    first = jnp.zeros((1, 1), I32)
    ranges = []
    for owner in range(8):
        count = table_ref[owner * 16 + 12 : owner * 16 + 13, 0:1]
        ranges.append((first, count))
        first = first + count
    return ranges


def segment_kernel(table_ref, row_ref, slot_ref, cot_ref, keep_ref, send_ref, wide, hot):
    z, core = lax.axis_index("z"), lax.axis_index("core")
    owner = row_ref[...]
    place = slot_ref[...]
    for index, (first, _) in enumerate(owner_ranges(table_ref)):
        place = jnp.where(owner == index, place + first, place)
    place = place ^ (core << 9)
    quarter = ((place >> 10) - z) & 3
    inner = place & 1023
    quarter_t = quarter.T
    ids = lax.broadcasted_iota(I32, (1024, 128), 0)
    for chunk in range(32):
        rows = slice(chunk * 128, chunk * 128 + 128)
        column = jnp.broadcast_to(quarter_t[:, chunk : chunk + 1], (128, 128))
        cot = cot_ref[rows, :].astype(F32)
        for part in range(4):
            wide[rows, part * 128 : part * 128 + 128] = jnp.where(column == part, cot, 0.0).astype(BF16)
        hot[:, rows] = jnp.where(inner[chunk : chunk + 1, :] == ids, 1.0, 0.0).astype(BF16)
    for pair in range(2):
        total = jnp.dot(hot[...], wide[:, pair * 256 : pair * 256 + 256], preferred_element_type=F32)
        for sub in range(2):
            part = pair * 2 + sub
            rows = slice(part * 512, part * 512 + 512)
            cols = slice(sub * 128, sub * 128 + 128)
            keep_ref[rows, :] = total[0:512, cols]
            send_ref[rows, :] = total[512:1024, cols].astype(BF16)


def join_kernel(keep_ref, got_ref, after_ref, own_ref, one_ref, two_ref, three_ref):
    own_ref[...] = keep_ref[0:512, :] + got_ref[0:512, :].astype(F32)
    for part, out in enumerate((one_ref, two_ref, three_ref), 1):
        rows = slice(part * 512, part * 512 + 512)
        out[...] = (keep_ref[rows, :] + got_ref[rows, :].astype(F32)).astype(BF16)


def total_kernel(own_ref, one_ref, two_ref, three_ref, after_ref, out_ref):
    total = own_ref[...] + one_ref[...].astype(F32) + two_ref[...].astype(F32) + three_ref[...].astype(F32)
    out_ref[...] = total.astype(BF16)


def mish_parts(value):
    e = jnp.exp(jnp.minimum(value, 20.0))
    n = e * (e + 2.0)
    inverse = 1.0 / (n + 2.0)
    tanh_soft = n * inverse
    twice = inverse + inverse
    return value * tanh_soft, tanh_soft + (value * (n - e)) * (twice * twice)


def pack_kernel(count_ref, ids_ref, cot_ref, row_ref, slot_ref,
                out_ref, cot_out, row_out, slot_out, ids, sems):
    pairs = ((ids_ref, ids), (cot_ref, cot_out), (row_ref, row_out), (slot_ref, slot_out))
    copies = [pltpu.make_async_copy(source, target, sems.at[index]) for index, (source, target) in enumerate(pairs)]
    for copy in copies:
        copy.start()
    copies[0].wait()
    for copy in range(8):
        out_ref[copy, 0:12, :] = ids[...]
        out_ref[copy, 12:16, :] = jnp.full((4, 128), count_ref[0], I32)
    for copy in copies[1:]:
        copy.wait()


def prepare_kernel(w_in_ref, w_mid_ref, w_out_ref, seeds_ref, after_ref,
                   w_in_t_ref, w_mid_t_ref, w_out_on_chip_ref, seeds_t_ref):
    for part in range(4):
        cols = slice(part * 256, part * 256 + 256)
        w_in_t_ref[cols, :] = w_in_ref[:, cols].T
        w_mid_t_ref[cols, :] = w_mid_ref[:, cols].T
    w_out_on_chip_ref[...] = w_out_ref[...]
    seeds_t_ref[...] = jnp.concatenate([seeds_ref[...], jnp.zeros((5, WIDTH), I32)], axis=0).T


def find_ids(z, core, table_ref):
    line = lax.broadcasted_iota(I32, (1, WIDTH), 1)
    place = z * 1024 + (line ^ (core << 9))
    where_at = jnp.zeros((1, WIDTH), I32)
    for index, (first, count) in enumerate(owner_ranges(table_ref)):
        inside = (place >= first) & (place < first + count)
        where_at = jnp.where(inside, place - first + index * 2048, where_at)
    sub = lax.broadcasted_iota(I32, (128, WIDTH), 0)
    pick = jnp.where((where_at >> 7) == sub, 1.0, 0.0).astype(BF16)
    table = table_ref[...].T
    found = jnp.zeros((128, WIDTH), F32)
    for shift_by in (0, 8, 16):
        piece = ((table >> shift_by) & 255).astype(F32).astype(BF16)
        found += jnp.dot(piece, pick, preferred_element_type=F32) * float(1 << shift_by)
    return jnp.sum(jnp.where((where_at & 127) == sub, found, 0.0), axis=0, keepdims=True).astype(I32)


def forward_kernel(table_ref, after_ref, seeds_ref, w_in_ref, w_mid_ref,
                   slope_one_ref, slope_two_ref, own_ref, send_ref, other_ref, codes, enc, one, two):
    z, core = lax.axis_index("z"), lax.axis_index("core")
    ids = find_ids(z, core, table_ref)
    low = (ids >> 16) * 15 + (ids & 65535)
    over = low >= PRIME
    high = (ids >> 16) + jnp.where(over, 1, 0)
    codes[0:1, :] = jnp.where(over, low - PRIME, low)
    codes[1:2, :] = jnp.where(high >= HIGH_PRIME, high - HIGH_PRIME, high)
    def encode(rows, cols):
        first, second, offset = (seeds_ref[rows, index : index + 1] for index in range(3))
        mix = first * codes[0:1, cols] + (second * codes[1:2, cols] + offset)
        mix = lax.shift_right_logical(mix, 16) * 15 + (mix & 65535)
        mix = (mix >> 16) * 15 + (mix & 65535)
        mix = jnp.where(mix >= PRIME, mix - PRIME, mix)
        return (mix.astype(F32) * (2.0 / 65520.0) - 1.0).astype(BF16)

    for block in range(2):
        cols = slice(block * 256, block * 256 + 256)
        for part in range(4):
            rows = slice(part * 256, part * 256 + 256)
            enc[rows, cols] = encode(rows, cols)
        for weights, source, target, slopes in (
            (w_in_ref, enc, one, slope_one_ref), (w_mid_ref, one, two, slope_two_ref)):
            for part in range(4):
                rows = slice(part * 256, part * 256 + 256)
                act, slope = mish_parts(jnp.dot(weights[rows, :], source[:, cols], preferred_element_type=F32))
                target[rows, cols] = act.astype(BF16)
                slopes[rows, cols] = slope
    for part in range(4):
        mine = pl.ds(pl.multiple_of(core * 128 + part * 256, 128), 128)
        theirs = pl.ds(pl.multiple_of((core ^ 1) * 128 + part * 256, 128), 128)
        for layer, source in enumerate((enc, one, two)):
            start = layer * 512 + part * 128
            own_ref[start : start + 128, :] = source[mine, :]
            if layer:
                send_ref[start - 512 : start - 384, :] = source[theirs, :]
        other_ref[part * 128 : part * 128 + 128, :] = encode(mine, slice(512, 1024))


NT = (((1,), (1,)), ((), ()))
TILES = tuple(slice(index * 256, index * 256 + 256) for index in range(4))


def delta_two_kernel(grad_ref, slope_ref, w_out_ref, delta_ref):
    for rows in TILES:
        back = lax.dot_general(w_out_ref[rows, :], grad_ref[...], NT, preferred_element_type=F32)
        delta_ref[rows, :] = (back * slope_ref[rows, :]).astype(BF16)
    delta_ref[1024:1152, :] = grad_ref[...].astype(F32).T.astype(BF16)


def delta_one_kernel(delta_two_ref, slope_ref, w_mid_ref, delta_ref):
    for rows in TILES:
        back = jnp.dot(w_mid_ref[rows, :], delta_two_ref[0:1024, :], preferred_element_type=F32)
        delta_ref[rows, :] = (back * slope_ref[rows, :]).astype(BF16)


def over_slots(own, delta, got, got_delta):
    return (lax.dot_general(own, delta, NT, preferred_element_type=F32)
            + lax.dot_general(got, got_delta, NT, preferred_element_type=F32))


def weights_two_kernel(own_ref, delta_ref, got_ref, got_delta_ref, keep_ref, one_ref, two_ref, three_ref, total):
    for cols in TILES:
        total[:, cols] = over_slots(
            own_ref[512:1024, :], delta_ref[cols, :], got_ref[0:512, :], got_delta_ref[cols, :])
    total[:, 1024:1152] = over_slots(
        own_ref[1024:1536, :], delta_ref[1024:1152, :], got_ref[512:1024, :], got_delta_ref[1024:1152, :])
    z = lax.axis_index("z")
    for step, out_ref in enumerate((keep_ref, one_ref, two_ref, three_ref)):
        rows = pl.ds(pl.multiple_of(((z + step) & 3) * 128, 128), 128)
        out_ref[...] = total[rows, :].astype(out_ref.dtype)


def weights_one_kernel(own_ref, delta_ref, other_ref, got_delta_ref, after_ref, out_ref):
    for cols in TILES:
        value = over_slots(own_ref[0:512, :], delta_ref[cols, :], other_ref[...], got_delta_ref[cols, :])
        out_ref[:, cols] = jnp.concatenate(
            [value[chip * 8 : chip * 8 + 8, :] for chip in BY_COLUMN], axis=0).astype(BF16)


def sum_columns_kernel(pieces_ref, keep_ref, one_ref, two_ref, three_ref, total):
    z = lax.axis_index("z")
    for col in range(0, 1024, 128):
        cols = slice(col, col + 128)
        total[:, cols] = sum(pieces_ref[piece * 32 : piece * 32 + 32, cols].astype(F32) for piece in range(16))
    for step, out_ref in enumerate((keep_ref, one_ref, two_ref, three_ref)):
        out_ref[...] = total[pl.ds(pl.multiple_of(((z + step) & 3) * 8, 8), 8), :]


def sum_rows_kernel(keep_ref, one_ref, two_ref, three_ref, after_ref, out_ref):
    total = keep_ref[...] + one_ref[...].astype(F32) + two_ref[...].astype(F32) + three_ref[...].astype(F32)
    out_ref[...] = total.astype(BF16)


def last_kernel(keep_ref, one_ref, two_ref, three_ref, pieces_ref, in_ref, mid_ref, last_ref):
    in_ref[...] = (keep_ref[...] + one_ref[...]) + (two_ref[...] + three_ref[...])
    for start, out_ref in ((0, mid_ref), (1024, last_ref)):
        for col in range(0, out_ref.shape[1], 128):
            cols = slice(start + col, start + col + 128)
            total = sum(pieces_ref[piece * 16 : piece * 16 + 16, cols].astype(F32) for piece in range(8))
            out_ref[:, col : col + 128] = total[0:8, :] + total[8:16, :]


def shift(steps):
    return [(index, (index + steps) % 4) for index in range(4)]


SWAP = [(0, 1), (1, 0)]


def per_device(cotangent, owner_row, owner_slot, counts, unique_ids, hash_seeds, w_in, w_mid, w_out):
    shape = jax.ShapeDtypeStruct

    anywhere = pl.BlockSpec(memory_space=pl.ANY)
    with jax.named_scope("gather_ids"):
        copies, cot, rows, slots = pl.pallas_call(
            pack_kernel,
            out_shape=(shape((8, 16, 128), I32), shape((LOOKUPS, EMBED), BF16),
                       shape((32, 128), I32), shape((32, 128), I32)),
            in_specs=[pl.BlockSpec(memory_space=pltpu.SMEM)] + [pl.BlockSpec(memory_space=pltpu.HBM)] * 4,
            out_specs=tuple(vmem(4)),
            scratch_shapes=[pltpu.VMEM((12, 128), I32), pltpu.SemaphoreType.DMA((4,))],
            compiler_params=params(PACK_LIMIT),
            name="pack_ids",
        )(counts, *(pltpu.with_memory_space_constraint(value, pltpu.HBM) for value in (
            unique_ids.reshape(12, 128), cotangent, owner_row.reshape(32, 128), owner_slot.reshape(32, 128))))
        table = lax.all_to_all(copies, ("z", "core"), split_axis=0, concat_axis=0, tiled=True).reshape(128, 128)

    keep, send = pl.pallas_call(
        segment_kernel,
        out_shape=(shape((2048, EMBED), F32), shape((2048, EMBED), BF16)),
        in_specs=vmem(4),
        out_specs=tuple(vmem(2)),
        scratch_shapes=[pltpu.VMEM((LOOKUPS, 512), BF16), pltpu.VMEM((1024, LOOKUPS), BF16)],
        compiler_params=params(),
        cost_estimate=pl.CostEstimate(flops=2 * 1024 * 4096 * 512, bytes_accessed=1 << 22, transcendentals=0),
        name="segment_sums",
    )(table, rows, slots, cot)

    with jax.named_scope("exchange_grads"):
        got = lax.ppermute(send, "core", SWAP)
        w_in_t, w_mid_t, w_out, seeds_t = pl.pallas_call(
            prepare_kernel,
            out_shape=(shape((WIDTH, WIDTH), BF16), shape((WIDTH, WIDTH), BF16),
                       shape((WIDTH, EMBED), BF16), shape((WIDTH, 8), I32)),
            in_specs=vmem(4) + [anywhere],
            out_specs=tuple(vmem(4)),
            compiler_params=params(),
            name="transpose_weights",
        )(w_in, w_mid, w_out, hash_seeds, send)
        own, one, two, three = pl.pallas_call(
            join_kernel,
            out_shape=(shape((512, EMBED), F32),) + (shape((512, EMBED), BF16),) * 3,
            in_specs=vmem(2) + [anywhere],
            out_specs=tuple(vmem(4)),
            compiler_params=params(),
            name="join_cores",
        )(keep, got, seeds_t)
        parts = [lax.ppermute(part, "z", shift(step)) for step, part in ((2, two), (1, one), (3, three))]

    slope_one, slope_two, own_units, send_units, other_enc = pl.pallas_call(
        forward_kernel,
        out_shape=(shape((WIDTH, SHARE), F32),) * 2 + (
            shape((3 * 512, SHARE), BF16), shape((2 * 512, SHARE), BF16), shape((512, SHARE), BF16)),
        in_specs=vmem(1) + [anywhere] + vmem(3),
        out_specs=tuple(vmem(5)),
        scratch_shapes=[pltpu.VMEM((8, WIDTH), I32)] + [pltpu.VMEM((WIDTH, SHARE), BF16)] * 3,
        compiler_params=params(),
        cost_estimate=pl.CostEstimate(flops=4 * 1024 ** 3, bytes_accessed=1 << 24, transcendentals=1 << 21),
        name="forward",
    )(table, one, seeds_t, w_in_t, w_mid_t)
    got_units = lax.ppermute(send_units, "core", SWAP)

    with jax.named_scope("grad_use"):
        grads = pl.pallas_call(
            total_kernel,
            out_shape=shape((SHARE, EMBED), BF16),
            in_specs=vmem(4) + [anywhere],
            out_specs=vmem(1)[0],
            compiler_params=params(),
            name="total_grads",
        )(own, *parts, own_units)

    with jax.named_scope("backward"):
        delta_two = pl.pallas_call(
            delta_two_kernel,
            out_shape=shape((1152, SHARE), BF16),
            in_specs=vmem(3),
            out_specs=vmem(1)[0],
            compiler_params=params(),
            name="delta_two",
        )(grads, slope_two, w_out)
        got_delta_two = lax.ppermute(delta_two, "core", SWAP)
        delta_one = pl.pallas_call(
            delta_one_kernel,
            out_shape=shape((WIDTH, SHARE), BF16),
            in_specs=vmem(3),
            out_specs=vmem(1)[0],
            compiler_params=params(),
            cost_estimate=pl.CostEstimate(flops=20 * 1024 ** 3, bytes_accessed=1 << 25, transcendentals=0),
            name="delta_one",
        )(delta_two, slope_one, w_mid)
        got_delta_one = lax.ppermute(delta_one, "core", SWAP)

    with jax.named_scope("sum_devices"):
        keep_two, *pieces = pl.pallas_call(
            weights_two_kernel,
            out_shape=(shape((128, 1152), F32),) + (shape((128, 1152), BF16),) * 3,
            in_specs=vmem(4),
            out_specs=tuple(vmem(4)),
            scratch_shapes=[pltpu.VMEM((512, 1152), F32)],
            compiler_params=params(),
            name="weights_two",
        )(own_units, delta_two, got_units, got_delta_two)
        rows_two = [lax.ppermute(pieces[step - 1], "z", shift(step)) for step in (2, 1, 3)]
        out_one = pl.pallas_call(
            weights_one_kernel,
            out_shape=shape((512, 1024), BF16),
            in_specs=vmem(4) + [anywhere],
            out_specs=vmem(1)[0],
            compiler_params=params(),
            name="weights_one",
        )(own_units, delta_one, other_enc, got_delta_one, pieces[0])
        columns_one = lax.all_to_all(out_one, ("x", "y"), split_axis=0, concat_axis=0, tiled=True)
        keep_one, *pieces = pl.pallas_call(
            sum_columns_kernel,
            out_shape=(shape((8, 1024), F32),) * 4,
            in_specs=vmem(1),
            out_specs=tuple(vmem(4)),
            scratch_shapes=[pltpu.VMEM((32, 1024), F32)],
            compiler_params=params(),
            name="sum_columns",
        )(columns_one)
        rows_one = [lax.ppermute(pieces[step - 1], "z", shift(step)) for step in (2, 1, 3)]
        out_two = pl.pallas_call(
            sum_rows_kernel,
            out_shape=shape((128, 1152), BF16),
            in_specs=vmem(4) + [anywhere],
            out_specs=vmem(1)[0],
            compiler_params=params(),
            name="sum_rows",
        )(keep_two, *rows_two, pieces[0])
        columns_two = lax.all_to_all(out_two, ("x", "y"), split_axis=0, concat_axis=0, tiled=True)
        return pl.pallas_call(
            last_kernel,
            out_shape=(shape((8, 1024), F32), shape((8, 1024), F32), shape((8, EMBED), F32)),
            in_specs=vmem(5),
            out_specs=tuple(vmem(3)),
            compiler_params=params(),
            name="last_sums",
        )(keep_one, *rows_one, columns_two)


def solution(mesh):
    fine = Mesh(mesh.devices.reshape(4, 2, 4, 4), ALL)
    split = P(ALL)
    rows = P(ALL, None)
    return jax.shard_map(
        per_device, mesh=fine, in_specs=(rows, split, split, split, split, P(), P(), P(), P()),
        out_specs=(rows, rows, rows), check_vma=False)
```

```python
import jax
import jax.numpy as jnp
from jax import lax
from jax.experimental import pallas as pl
from jax.experimental.pallas import tpu as pltpu
from jax.sharding import Mesh, PartitionSpec as P

PRIME = 65521
HIGH_PRIME = 32749
SLOTS = 1536
LOOKUPS = 4096
WIDTH = 1024
EMBED = 128
SHARE = 512
ALL = ("z", "core", "x", "y")
VMEM_LIMIT = 24 * 1024 * 1024
PACK_LIMIT = 24 * 1024 * 1024
BY_COLUMN = tuple(z * 16 + column for column in range(16) for z in range(4))
BF16 = jnp.bfloat16
F32 = jnp.float32
I32 = jnp.int32


def vmem(count):
    return [pl.BlockSpec(memory_space=pltpu.VMEM)] * count


def params(limit=VMEM_LIMIT):
    return pltpu.CompilerParams(vmem_limit_bytes=limit)


def owner_ranges(table_ref):
    first = jnp.zeros((1, 1), I32)
    ranges = []
    for owner in range(8):
        count = table_ref[owner * 16 + 12 : owner * 16 + 13, 0:1]
        ranges.append((first, count))
        first = first + count
    return ranges


def segment_kernel(table_ref, row_ref, slot_ref, cot_ref, keep_ref, send_ref, wide, hot):
    z, core = lax.axis_index("z"), lax.axis_index("core")
    owner = row_ref[...]
    place = slot_ref[...]
    for index, (first, _) in enumerate(owner_ranges(table_ref)):
        place = jnp.where(owner == index, place + first, place)
    place = place ^ (core << 9)
    quarter = ((place >> 10) - z) & 3
    inner = place & 1023
    quarter_t = quarter.T
    ids = lax.broadcasted_iota(I32, (1024, 128), 0)
    for chunk in range(32):
        rows = slice(chunk * 128, chunk * 128 + 128)
        column = jnp.broadcast_to(quarter_t[:, chunk : chunk + 1], (128, 128))
        cot = cot_ref[rows, :].astype(F32)
        for part in range(4):
            wide[rows, part * 128 : part * 128 + 128] = jnp.where(column == part, cot, 0.0).astype(BF16)
        hot[:, rows] = jnp.where(inner[chunk : chunk + 1, :] == ids, 1.0, 0.0).astype(BF16)
    for pair in range(2):
        total = jnp.dot(hot[...], wide[:, pair * 256 : pair * 256 + 256], preferred_element_type=F32)
        for sub in range(2):
            part = pair * 2 + sub
            rows = slice(part * 512, part * 512 + 512)
            cols = slice(sub * 128, sub * 128 + 128)
            keep_ref[rows, :] = total[0:512, cols]
            send_ref[rows, :] = total[512:1024, cols].astype(BF16)


def join_kernel(keep_ref, got_ref, after_ref, own_ref, one_ref, two_ref, three_ref):
    own_ref[...] = keep_ref[0:512, :] + got_ref[0:512, :].astype(F32)
    for part, out in enumerate((one_ref, two_ref, three_ref), 1):
        rows = slice(part * 512, part * 512 + 512)
        out[...] = (keep_ref[rows, :] + got_ref[rows, :].astype(F32)).astype(BF16)


def total_kernel(own_ref, one_ref, two_ref, three_ref, after_ref, out_ref):
    total = own_ref[...] + one_ref[...].astype(F32) + two_ref[...].astype(F32) + three_ref[...].astype(F32)
    out_ref[...] = total.astype(BF16)


def mish_parts(value):
    e = jnp.exp(jnp.minimum(value, 20.0))
    n = e * (e + 2.0)
    inverse = 1.0 / (n + 2.0)
    tanh_soft = n * inverse
    twice = inverse + inverse
    return value * tanh_soft, tanh_soft + (value * (n - e)) * (twice * twice)


def pack_kernel(count_ref, ids_ref, cot_ref, row_ref, slot_ref,
                out_ref, cot_out, row_out, slot_out, ids, sems):
    pairs = ((ids_ref, ids), (cot_ref, cot_out), (row_ref, row_out), (slot_ref, slot_out))
    copies = [pltpu.make_async_copy(source, target, sems.at[index]) for index, (source, target) in enumerate(pairs)]
    for copy in copies:
        copy.start()
    copies[0].wait()
    for copy in range(8):
        out_ref[copy, 0:12, :] = ids[...]
        out_ref[copy, 12:16, :] = jnp.full((4, 128), count_ref[0], I32)
    for copy in copies[1:]:
        copy.wait()


def prepare_kernel(w_in_ref, w_mid_ref, w_out_ref, seeds_ref, after_ref,
                   w_in_t_ref, w_mid_t_ref, w_out_on_chip_ref, seeds_t_ref):
    for part in range(4):
        cols = slice(part * 256, part * 256 + 256)
        w_in_t_ref[cols, :] = w_in_ref[:, cols].T
        w_mid_t_ref[cols, :] = w_mid_ref[:, cols].T
    w_out_on_chip_ref[...] = w_out_ref[...]
    seeds_t_ref[...] = jnp.concatenate([seeds_ref[...], jnp.zeros((5, WIDTH), I32)], axis=0).T


def find_ids(z, core, table_ref):
    line = lax.broadcasted_iota(I32, (1, WIDTH), 1)
    place = z * 1024 + (line ^ (core << 9))
    where_at = jnp.zeros((1, WIDTH), I32)
    for index, (first, count) in enumerate(owner_ranges(table_ref)):
        inside = (place >= first) & (place < first + count)
        where_at = jnp.where(inside, place - first + index * 2048, where_at)
    sub = lax.broadcasted_iota(I32, (128, WIDTH), 0)
    pick = jnp.where((where_at >> 7) == sub, 1.0, 0.0).astype(BF16)
    table = table_ref[...].T
    found = jnp.zeros((128, WIDTH), F32)
    for shift_by in (0, 8, 16):
        piece = ((table >> shift_by) & 255).astype(F32).astype(BF16)
        found += jnp.dot(piece, pick, preferred_element_type=F32) * float(1 << shift_by)
    return jnp.sum(jnp.where((where_at & 127) == sub, found, 0.0), axis=0, keepdims=True).astype(I32)


def forward_kernel(table_ref, after_ref, seeds_ref, w_in_ref, w_mid_ref,
                   slope_one_ref, slope_two_ref, own_ref, send_ref, other_ref, codes, enc, one, two):
    z, core = lax.axis_index("z"), lax.axis_index("core")
    ids = find_ids(z, core, table_ref)
    low = (ids >> 16) * 15 + (ids & 65535)
    over = low >= PRIME
    high = (ids >> 16) + jnp.where(over, 1, 0)
    codes[0:1, :] = jnp.where(over, low - PRIME, low)
    codes[1:2, :] = jnp.where(high >= HIGH_PRIME, high - HIGH_PRIME, high)
    def encode(rows, cols):
        first, second, offset = (seeds_ref[rows, index : index + 1] for index in range(3))
        mix = first * codes[0:1, cols] + (second * codes[1:2, cols] + offset)
        mix = lax.shift_right_logical(mix, 16) * 15 + (mix & 65535)
        mix = (mix >> 16) * 15 + (mix & 65535)
        mix = jnp.where(mix >= PRIME, mix - PRIME, mix)
        return (mix.astype(F32) * (2.0 / 65520.0) - 1.0).astype(BF16)

    for block in range(2):
        cols = slice(block * 256, block * 256 + 256)
        for part in range(4):
            rows = slice(part * 256, part * 256 + 256)
            enc[rows, cols] = encode(rows, cols)
        for weights, source, target, slopes in (
            (w_in_ref, enc, one, slope_one_ref), (w_mid_ref, one, two, slope_two_ref)):
            for part in range(4):
                rows = slice(part * 256, part * 256 + 256)
                act, slope = mish_parts(jnp.dot(weights[rows, :], source[:, cols], preferred_element_type=F32))
                target[rows, cols] = act.astype(BF16)
                slopes[rows, cols] = slope
    for part in range(4):
        mine = pl.ds(pl.multiple_of(core * 128 + part * 256, 128), 128)
        theirs = pl.ds(pl.multiple_of((core ^ 1) * 128 + part * 256, 128), 128)
        for layer, source in enumerate((enc, one, two)):
            start = layer * 512 + part * 128
            own_ref[start : start + 128, :] = source[mine, :]
            if layer:
                send_ref[start - 512 : start - 384, :] = source[theirs, :]
        other_ref[part * 128 : part * 128 + 128, :] = encode(mine, slice(512, 1024))


NT = (((1,), (1,)), ((), ()))
TILES = tuple(slice(index * 256, index * 256 + 256) for index in range(4))


def delta_two_kernel(grad_ref, slope_ref, w_out_ref, delta_ref):
    for rows in TILES:
        back = lax.dot_general(w_out_ref[rows, :], grad_ref[...], NT, preferred_element_type=F32)
        delta_ref[rows, :] = (back * slope_ref[rows, :]).astype(BF16)
    delta_ref[1024:1152, :] = grad_ref[...].astype(F32).T.astype(BF16)


def delta_one_kernel(delta_two_ref, slope_ref, w_mid_ref, delta_ref):
    for rows in TILES:
        back = jnp.dot(w_mid_ref[rows, :], delta_two_ref[0:1024, :], preferred_element_type=F32)
        delta_ref[rows, :] = (back * slope_ref[rows, :]).astype(BF16)


def over_slots(own, delta, got, got_delta):
    return (lax.dot_general(own, delta, NT, preferred_element_type=F32)
            + lax.dot_general(got, got_delta, NT, preferred_element_type=F32))


def weights_two_kernel(own_ref, delta_ref, got_ref, got_delta_ref, keep_ref, one_ref, two_ref, three_ref, total):
    for cols in TILES:
        total[:, cols] = over_slots(
            own_ref[512:1024, :], delta_ref[cols, :], got_ref[0:512, :], got_delta_ref[cols, :])
    z = lax.axis_index("z")
    for step, out_ref in enumerate((keep_ref, one_ref, two_ref, three_ref)):
        rows = pl.ds(pl.multiple_of(((z + step) & 3) * 128, 128), 128)
        out_ref[...] = total[rows, :].astype(out_ref.dtype)


def by_column(value):
    return jnp.concatenate([value[chip * 8 : chip * 8 + 8, :] for chip in BY_COLUMN], axis=0).astype(BF16)


def weights_one_kernel(own_ref, delta_ref, other_ref, got_delta_ref, delta_two_ref, got_ref, got_delta_two_ref,
                       after_ref, out_ref):
    for cols in TILES:
        out_ref[:, cols] = by_column(
            over_slots(own_ref[0:512, :], delta_ref[cols, :], other_ref[...], got_delta_ref[cols, :]))
    out_ref[:, 1024:1152] = by_column(over_slots(
        own_ref[1024:1536, :], delta_two_ref[1024:1152, :], got_ref[512:1024, :], got_delta_two_ref[1024:1152, :]))


def sum_columns_kernel(pieces_ref, after_ref, keep_ref, one_ref, two_ref, three_ref, total):
    z = lax.axis_index("z")
    for col in range(0, 1152, 128):
        cols = slice(col, col + 128)
        total[:, cols] = sum(pieces_ref[piece * 32 : piece * 32 + 32, cols].astype(F32) for piece in range(16))
    for step, out_ref in enumerate((keep_ref, one_ref, two_ref, three_ref)):
        out_ref[...] = total[pl.ds(pl.multiple_of(((z + step) & 3) * 8, 8), 8), :]


def sum_rows_kernel(keep_ref, one_ref, two_ref, three_ref, out_ref):
    total = keep_ref[...] + one_ref[...].astype(F32) + two_ref[...].astype(F32) + three_ref[...].astype(F32)
    out_ref[...] = total.astype(BF16)


def last_kernel(keep_ref, one_ref, two_ref, three_ref, pieces_ref, in_ref, mid_ref, last_ref):
    for cols, out_ref in ((slice(0, 1024), in_ref), (slice(1024, 1152), last_ref)):
        out_ref[...] = (keep_ref[:, cols] + one_ref[:, cols]) + (two_ref[:, cols] + three_ref[:, cols])
    for col in range(0, 1024, 128):
        cols = slice(col, col + 128)
        total = sum(pieces_ref[piece * 16 : piece * 16 + 16, cols].astype(F32) for piece in range(8))
        mid_ref[:, cols] = total[0:8, :] + total[8:16, :]


def shift(steps):
    return [(index, (index + steps) % 4) for index in range(4)]


SWAP = [(0, 1), (1, 0)]


def per_device(cotangent, owner_row, owner_slot, counts, unique_ids, hash_seeds, w_in, w_mid, w_out):
    shape = jax.ShapeDtypeStruct

    anywhere = pl.BlockSpec(memory_space=pl.ANY)
    with jax.named_scope("gather_ids"):
        copies, cot, rows, slots = pl.pallas_call(
            pack_kernel,
            out_shape=(shape((8, 16, 128), I32), shape((LOOKUPS, EMBED), BF16),
                       shape((32, 128), I32), shape((32, 128), I32)),
            in_specs=[pl.BlockSpec(memory_space=pltpu.SMEM)] + [pl.BlockSpec(memory_space=pltpu.HBM)] * 4,
            out_specs=tuple(vmem(4)),
            scratch_shapes=[pltpu.VMEM((12, 128), I32), pltpu.SemaphoreType.DMA((4,))],
            compiler_params=params(PACK_LIMIT),
            name="pack_ids",
        )(counts, *(pltpu.with_memory_space_constraint(value, pltpu.HBM) for value in (
            unique_ids.reshape(12, 128), cotangent, owner_row.reshape(32, 128), owner_slot.reshape(32, 128))))
        table = lax.all_to_all(copies, ("z", "core"), split_axis=0, concat_axis=0, tiled=True).reshape(128, 128)

    keep, send = pl.pallas_call(
        segment_kernel,
        out_shape=(shape((2048, EMBED), F32), shape((2048, EMBED), BF16)),
        in_specs=vmem(4),
        out_specs=tuple(vmem(2)),
        scratch_shapes=[pltpu.VMEM((LOOKUPS, 512), BF16), pltpu.VMEM((1024, LOOKUPS), BF16)],
        compiler_params=params(),
        cost_estimate=pl.CostEstimate(flops=2 * 1024 * 4096 * 512, bytes_accessed=1 << 22, transcendentals=0),
        name="segment_sums",
    )(table, rows, slots, cot)

    with jax.named_scope("exchange_grads"):
        got = lax.ppermute(send, "core", SWAP)
        w_in_t, w_mid_t, w_out, seeds_t = pl.pallas_call(
            prepare_kernel,
            out_shape=(shape((WIDTH, WIDTH), BF16), shape((WIDTH, WIDTH), BF16),
                       shape((WIDTH, EMBED), BF16), shape((WIDTH, 8), I32)),
            in_specs=vmem(4) + [anywhere],
            out_specs=tuple(vmem(4)),
            compiler_params=params(),
            name="transpose_weights",
        )(w_in, w_mid, w_out, hash_seeds, send)
        own, one, two, three = pl.pallas_call(
            join_kernel,
            out_shape=(shape((512, EMBED), F32),) + (shape((512, EMBED), BF16),) * 3,
            in_specs=vmem(2) + [anywhere],
            out_specs=tuple(vmem(4)),
            compiler_params=params(),
            name="join_cores",
        )(keep, got, seeds_t)
        parts = [lax.ppermute(part, "z", shift(step)) for step, part in ((2, two), (1, one), (3, three))]

    slope_one, slope_two, own_units, send_units, other_enc = pl.pallas_call(
        forward_kernel,
        out_shape=(shape((WIDTH, SHARE), F32),) * 2 + (
            shape((3 * 512, SHARE), BF16), shape((2 * 512, SHARE), BF16), shape((512, SHARE), BF16)),
        in_specs=vmem(1) + [anywhere] + vmem(3),
        out_specs=tuple(vmem(5)),
        scratch_shapes=[pltpu.VMEM((8, WIDTH), I32)] + [pltpu.VMEM((WIDTH, SHARE), BF16)] * 3,
        compiler_params=params(),
        cost_estimate=pl.CostEstimate(flops=4 * 1024 ** 3, bytes_accessed=1 << 24, transcendentals=1 << 21),
        name="forward",
    )(table, one, seeds_t, w_in_t, w_mid_t)
    got_units = lax.ppermute(send_units, "core", SWAP)

    with jax.named_scope("grad_use"):
        grads = pl.pallas_call(
            total_kernel,
            out_shape=shape((SHARE, EMBED), BF16),
            in_specs=vmem(4) + [anywhere],
            out_specs=vmem(1)[0],
            compiler_params=params(),
            name="total_grads",
        )(own, *parts, own_units)

    with jax.named_scope("backward"):
        delta_two = pl.pallas_call(
            delta_two_kernel,
            out_shape=shape((1152, SHARE), BF16),
            in_specs=vmem(3),
            out_specs=vmem(1)[0],
            compiler_params=params(),
            name="delta_two",
        )(grads, slope_two, w_out)
        got_delta_two = lax.ppermute(delta_two, "core", SWAP)
        delta_one = pl.pallas_call(
            delta_one_kernel,
            out_shape=shape((WIDTH, SHARE), BF16),
            in_specs=vmem(3),
            out_specs=vmem(1)[0],
            compiler_params=params(),
            cost_estimate=pl.CostEstimate(flops=20 * 1024 ** 3, bytes_accessed=1 << 25, transcendentals=0),
            name="delta_one",
        )(delta_two, slope_one, w_mid)
        got_delta_one = lax.ppermute(delta_one, "core", SWAP)

    with jax.named_scope("sum_devices"):
        keep_two, *pieces = pl.pallas_call(
            weights_two_kernel,
            out_shape=(shape((128, 1024), F32),) + (shape((128, 1024), BF16),) * 3,
            in_specs=vmem(4),
            out_specs=tuple(vmem(4)),
            scratch_shapes=[pltpu.VMEM((512, 1024), F32)],
            compiler_params=params(),
            name="weights_two",
        )(own_units, delta_two, got_units, got_delta_two)
        rows_two = [lax.ppermute(pieces[step - 1], "z", shift(step)) for step in (2, 1, 3)]
        out_one = pl.pallas_call(
            weights_one_kernel,
            out_shape=shape((512, 1152), BF16),
            in_specs=vmem(7) + [anywhere],
            out_specs=vmem(1)[0],
            compiler_params=params(),
            name="weights_one",
        )(own_units, delta_one, other_enc, got_delta_one, delta_two, got_units, got_delta_two, pieces[0])
        columns_one = lax.all_to_all(out_one, ("x", "y"), split_axis=0, concat_axis=0, tiled=True)
        out_two = pl.pallas_call(
            sum_rows_kernel,
            out_shape=shape((128, 1024), BF16),
            in_specs=vmem(4),
            out_specs=vmem(1)[0],
            compiler_params=params(),
            name="sum_rows",
        )(keep_two, *rows_two)
        keep_one, *pieces = pl.pallas_call(
            sum_columns_kernel,
            out_shape=(shape((8, 1152), F32),) * 4,
            in_specs=vmem(1) + [anywhere],
            out_specs=tuple(vmem(4)),
            scratch_shapes=[pltpu.VMEM((32, 1152), F32)],
            compiler_params=params(),
            name="sum_columns",
        )(columns_one, out_two)
        rows_one = [lax.ppermute(pieces[step - 1], "z", shift(step)) for step in (2, 1, 3)]
        columns_two = lax.all_to_all(out_two, ("x", "y"), split_axis=0, concat_axis=0, tiled=True)
        return pl.pallas_call(
            last_kernel,
            out_shape=(shape((8, 1024), F32), shape((8, 1024), F32), shape((8, EMBED), F32)),
            in_specs=vmem(5),
            out_specs=tuple(vmem(3)),
            compiler_params=params(),
            name="last_sums",
        )(keep_one, *rows_one, columns_two)


def solution(mesh):
    fine = Mesh(mesh.devices.reshape(4, 2, 4, 4), ALL)
    split = P(ALL)
    rows = P(ALL, None)
    return jax.shard_map(
        per_device, mesh=fine, in_specs=(rows, split, split, split, split, P(), P(), P(), P()),
        out_specs=(rows, rows, rows), check_vma=False)
```

```python
import jax
import jax.numpy as jnp
from jax import lax
from jax.experimental import pallas as pl
from jax.experimental.pallas import tpu as pltpu
from jax.sharding import Mesh, PartitionSpec as P

PRIME = 65521
HIGH_PRIME = 32749
SLOTS = 1536
LOOKUPS = 4096
WIDTH = 1024
EMBED = 128
SHARE = 512
ALL = ("z", "core", "x", "y")
VMEM_LIMIT = 24 * 1024 * 1024
PACK_LIMIT = 24 * 1024 * 1024
BY_COLUMN = tuple(z * 16 + column for column in range(16) for z in range(4))
BF16 = jnp.bfloat16
F32 = jnp.float32
I32 = jnp.int32


def vmem(count):
    return [pl.BlockSpec(memory_space=pltpu.VMEM)] * count


def params(limit=VMEM_LIMIT):
    return pltpu.CompilerParams(vmem_limit_bytes=limit)


def owner_ranges(table_ref):
    first = jnp.zeros((1, 1), I32)
    ranges = []
    for owner in range(8):
        count = table_ref[owner * 16 + 12 : owner * 16 + 13, 0:1]
        ranges.append((first, count))
        first = first + count
    return ranges


def segment_kernel(table_ref, row_ref, slot_ref, cot_ref, keep_ref, send_ref, wide, hot):
    z, core = lax.axis_index("z"), lax.axis_index("core")
    owner = row_ref[...]
    place = slot_ref[...]
    for index, (first, _) in enumerate(owner_ranges(table_ref)):
        place = jnp.where(owner == index, place + first, place)
    place = place ^ (core << 9)
    quarter = ((place >> 10) - z) & 3
    inner = place & 1023
    quarter_t = quarter.T
    ids = lax.broadcasted_iota(I32, (1024, 128), 0)
    for chunk in range(32):
        rows = slice(chunk * 128, chunk * 128 + 128)
        column = jnp.broadcast_to(quarter_t[:, chunk : chunk + 1], (128, 128))
        cot = cot_ref[rows, :].astype(F32)
        for part in range(4):
            wide[rows, part * 128 : part * 128 + 128] = jnp.where(column == part, cot, 0.0).astype(BF16)
        hot[:, rows] = jnp.where(inner[chunk : chunk + 1, :] == ids, 1.0, 0.0).astype(BF16)
    for pair in range(2):
        total = jnp.dot(hot[...], wide[:, pair * 256 : pair * 256 + 256], preferred_element_type=F32)
        for sub in range(2):
            part = pair * 2 + sub
            rows = slice(part * 512, part * 512 + 512)
            cols = slice(sub * 128, sub * 128 + 128)
            keep_ref[rows, :] = total[0:512, cols]
            send_ref[rows, :] = total[512:1024, cols].astype(BF16)


def join_kernel(keep_ref, got_ref, after_ref, own_ref, one_ref, two_ref, three_ref):
    own_ref[...] = keep_ref[0:512, :] + got_ref[0:512, :].astype(F32)
    for part, out in enumerate((one_ref, two_ref, three_ref), 1):
        rows = slice(part * 512, part * 512 + 512)
        out[...] = (keep_ref[rows, :] + got_ref[rows, :].astype(F32)).astype(BF16)


def total_kernel(own_ref, one_ref, two_ref, three_ref, after_ref, out_ref):
    total = own_ref[...] + one_ref[...].astype(F32) + two_ref[...].astype(F32) + three_ref[...].astype(F32)
    out_ref[...] = total.astype(BF16)


def mish_parts(value):
    e = jnp.exp(jnp.minimum(value, 20.0))
    n = e * (e + 2.0)
    inverse = 1.0 / (n + 2.0)
    tanh_soft = n * inverse
    twice = inverse + inverse
    return value * tanh_soft, tanh_soft + (value * (n - e)) * (twice * twice)


def pack_kernel(count_ref, ids_ref, cot_ref, row_ref, slot_ref,
                out_ref, cot_out, row_out, slot_out, ids, sems):
    pairs = ((ids_ref, ids), (cot_ref, cot_out), (row_ref, row_out), (slot_ref, slot_out))
    copies = [pltpu.make_async_copy(source, target, sems.at[index]) for index, (source, target) in enumerate(pairs)]
    for copy in copies:
        copy.start()
    copies[0].wait()
    for copy in range(8):
        out_ref[copy, 0:12, :] = ids[...]
        out_ref[copy, 12:16, :] = jnp.full((4, 128), count_ref[0], I32)
    for copy in copies[1:]:
        copy.wait()


def prepare_kernel(w_in_ref, w_mid_ref, w_out_ref, seeds_ref, after_ref,
                   w_in_t_ref, w_mid_t_ref, w_out_on_chip_ref, seeds_t_ref):
    for part in range(4):
        cols = slice(part * 256, part * 256 + 256)
        w_in_t_ref[cols, :] = w_in_ref[:, cols].T
        w_mid_t_ref[cols, :] = w_mid_ref[:, cols].T
    w_out_on_chip_ref[...] = w_out_ref[...]
    seeds_t_ref[...] = jnp.concatenate([seeds_ref[...], jnp.zeros((5, WIDTH), I32)], axis=0).T


def find_ids(z, core, table_ref):
    line = lax.broadcasted_iota(I32, (1, WIDTH), 1)
    place = z * 1024 + (line ^ (core << 9))
    where_at = jnp.zeros((1, WIDTH), I32)
    for index, (first, count) in enumerate(owner_ranges(table_ref)):
        inside = (place >= first) & (place < first + count)
        where_at = jnp.where(inside, place - first + index * 2048, where_at)
    sub = lax.broadcasted_iota(I32, (128, WIDTH), 0)
    pick = jnp.where((where_at >> 7) == sub, 1.0, 0.0).astype(BF16)
    table = table_ref[...].T
    found = jnp.zeros((128, WIDTH), F32)
    for shift_by in (0, 8, 16):
        piece = ((table >> shift_by) & 255).astype(F32).astype(BF16)
        found += jnp.dot(piece, pick, preferred_element_type=F32) * float(1 << shift_by)
    return jnp.sum(jnp.where((where_at & 127) == sub, found, 0.0), axis=0, keepdims=True).astype(I32)


def forward_kernel(table_ref, after_ref, seeds_ref, w_in_ref, w_mid_ref,
                   slope_one_ref, slope_two_ref, own_ref, send_ref, other_ref, codes, enc, one, two):
    z, core = lax.axis_index("z"), lax.axis_index("core")
    ids = find_ids(z, core, table_ref)
    low = (ids >> 16) * 15 + (ids & 65535)
    over = low >= PRIME
    high = (ids >> 16) + jnp.where(over, 1, 0)
    codes[0:1, :] = jnp.where(over, low - PRIME, low)
    codes[1:2, :] = jnp.where(high >= HIGH_PRIME, high - HIGH_PRIME, high)
    def encode(rows, cols):
        first, second, offset = (seeds_ref[rows, index : index + 1] for index in range(3))
        mix = first * codes[0:1, cols] + (second * codes[1:2, cols] + offset)
        mix = lax.shift_right_logical(mix, 16) * 15 + (mix & 65535)
        mix = (mix >> 16) * 15 + (mix & 65535)
        mix = jnp.where(mix >= PRIME, mix - PRIME, mix)
        return (mix.astype(F32) * (2.0 / 65520.0) - 1.0).astype(BF16)

    for block in range(2):
        cols = slice(block * 256, block * 256 + 256)
        for part in range(4):
            rows = slice(part * 256, part * 256 + 256)
            enc[rows, cols] = encode(rows, cols)
        for weights, source, target, slopes in (
            (w_in_ref, enc, one, slope_one_ref), (w_mid_ref, one, two, slope_two_ref)):
            for part in range(4):
                rows = slice(part * 256, part * 256 + 256)
                act, slope = mish_parts(jnp.dot(weights[rows, :], source[:, cols], preferred_element_type=F32))
                target[rows, cols] = act.astype(BF16)
                slopes[rows, cols] = slope
    for part in range(4):
        mine = pl.ds(pl.multiple_of(core * 128 + part * 256, 128), 128)
        theirs = pl.ds(pl.multiple_of((core ^ 1) * 128 + part * 256, 128), 128)
        for layer, source in enumerate((enc, one, two)):
            start = layer * 512 + part * 128
            own_ref[start : start + 128, :] = source[mine, :]
            if layer:
                send_ref[start - 512 : start - 384, :] = source[theirs, :]
        other_ref[part * 128 : part * 128 + 128, :] = encode(mine, slice(512, 1024))


NT = (((1,), (1,)), ((), ()))
TILES = tuple(slice(index * 256, index * 256 + 256) for index in range(4))


def delta_two_kernel(grad_ref, slope_ref, w_out_ref, delta_ref):
    for rows in TILES:
        back = lax.dot_general(w_out_ref[rows, :], grad_ref[...], NT, preferred_element_type=F32)
        delta_ref[rows, :] = (back * slope_ref[rows, :]).astype(BF16)
    delta_ref[1024:1152, :] = grad_ref[...].astype(F32).T.astype(BF16)


def delta_one_kernel(delta_two_ref, slope_ref, w_mid_ref, delta_ref):
    for rows in TILES:
        back = jnp.dot(w_mid_ref[rows, :], delta_two_ref[0:1024, :], preferred_element_type=F32)
        delta_ref[rows, :] = (back * slope_ref[rows, :]).astype(BF16)


def over_slots(own, delta, got, got_delta):
    return (lax.dot_general(own, delta, NT, preferred_element_type=F32)
            + lax.dot_general(got, got_delta, NT, preferred_element_type=F32))


def weights_two_kernel(own_ref, delta_ref, got_ref, got_delta_ref, keep_ref, one_ref, two_ref, three_ref, total):
    for cols in TILES:
        total[:, cols] = over_slots(
            own_ref[512:1024, :], delta_ref[cols, :], got_ref[0:512, :], got_delta_ref[cols, :])
    z = lax.axis_index("z")
    for step, out_ref in enumerate((keep_ref, one_ref, two_ref, three_ref)):
        rows = pl.ds(pl.multiple_of(((z + step) & 3) * 128, 128), 128)
        out_ref[...] = total[rows, :].astype(out_ref.dtype)


def by_column(value):
    return jnp.concatenate([value[chip * 8 : chip * 8 + 8, :] for chip in BY_COLUMN], axis=0).astype(BF16)


def weights_one_kernel(own_ref, delta_ref, other_ref, got_delta_ref, delta_two_ref, got_ref, got_delta_two_ref,
                       after_ref, out_ref, tiles, sems):
    copies = []

    def leave(cols):
        copies.append(pltpu.make_async_copy(tiles.at[:, cols], out_ref.at[:, cols], sems.at[len(copies)]))
        copies[-1].start()

    tiles[:, 1024:1152] = by_column(over_slots(
        own_ref[1024:1536, :], delta_two_ref[1024:1152, :], got_ref[512:1024, :], got_delta_two_ref[1024:1152, :]))
    leave(slice(1024, 1152))
    for cols in TILES:
        tiles[:, cols] = by_column(
            over_slots(own_ref[0:512, :], delta_ref[cols, :], other_ref[...], got_delta_ref[cols, :]))
        leave(cols)
    for copy in copies:
        copy.wait()


def sum_columns_kernel(pieces_ref, after_ref, keep_ref, one_ref, two_ref, three_ref, total):
    z = lax.axis_index("z")
    for col in range(0, 1152, 128):
        cols = slice(col, col + 128)
        total[:, cols] = sum(pieces_ref[piece * 32 : piece * 32 + 32, cols].astype(F32) for piece in range(16))
    for step, out_ref in enumerate((keep_ref, one_ref, two_ref, three_ref)):
        out_ref[...] = total[pl.ds(pl.multiple_of(((z + step) & 3) * 8, 8), 8), :]


def sum_rows_kernel(keep_ref, one_ref, two_ref, three_ref, out_ref):
    total = keep_ref[...] + one_ref[...].astype(F32) + two_ref[...].astype(F32) + three_ref[...].astype(F32)
    out_ref[...] = total.astype(BF16)


def last_kernel(keep_ref, one_ref, two_ref, three_ref, pieces_ref, in_ref, mid_ref, last_ref):
    for cols, out_ref in ((slice(0, 1024), in_ref), (slice(1024, 1152), last_ref)):
        out_ref[...] = (keep_ref[:, cols] + one_ref[:, cols]) + (two_ref[:, cols] + three_ref[:, cols])
    for col in range(0, 1024, 128):
        cols = slice(col, col + 128)
        total = sum(pieces_ref[piece * 16 : piece * 16 + 16, cols].astype(F32) for piece in range(8))
        mid_ref[:, cols] = total[0:8, :] + total[8:16, :]


def shift(steps):
    return [(index, (index + steps) % 4) for index in range(4)]


SWAP = [(0, 1), (1, 0)]


def per_device(cotangent, owner_row, owner_slot, counts, unique_ids, hash_seeds, w_in, w_mid, w_out):
    shape = jax.ShapeDtypeStruct

    anywhere = pl.BlockSpec(memory_space=pl.ANY)
    with jax.named_scope("gather_ids"):
        copies, cot, rows, slots = pl.pallas_call(
            pack_kernel,
            out_shape=(shape((8, 16, 128), I32), shape((LOOKUPS, EMBED), BF16),
                       shape((32, 128), I32), shape((32, 128), I32)),
            in_specs=[pl.BlockSpec(memory_space=pltpu.SMEM)] + [pl.BlockSpec(memory_space=pltpu.HBM)] * 4,
            out_specs=tuple(vmem(4)),
            scratch_shapes=[pltpu.VMEM((12, 128), I32), pltpu.SemaphoreType.DMA((4,))],
            compiler_params=params(PACK_LIMIT),
            name="pack_ids",
        )(counts, *(pltpu.with_memory_space_constraint(value, pltpu.HBM) for value in (
            unique_ids.reshape(12, 128), cotangent, owner_row.reshape(32, 128), owner_slot.reshape(32, 128))))
        table = lax.all_to_all(copies, ("z", "core"), split_axis=0, concat_axis=0, tiled=True).reshape(128, 128)

    keep, send = pl.pallas_call(
        segment_kernel,
        out_shape=(shape((2048, EMBED), F32), shape((2048, EMBED), BF16)),
        in_specs=vmem(4),
        out_specs=tuple(vmem(2)),
        scratch_shapes=[pltpu.VMEM((LOOKUPS, 512), BF16), pltpu.VMEM((1024, LOOKUPS), BF16)],
        compiler_params=params(),
        cost_estimate=pl.CostEstimate(flops=2 * 1024 * 4096 * 512, bytes_accessed=1 << 22, transcendentals=0),
        name="segment_sums",
    )(table, rows, slots, cot)

    with jax.named_scope("exchange_grads"):
        got = lax.ppermute(send, "core", SWAP)
        w_in_t, w_mid_t, w_out, seeds_t = pl.pallas_call(
            prepare_kernel,
            out_shape=(shape((WIDTH, WIDTH), BF16), shape((WIDTH, WIDTH), BF16),
                       shape((WIDTH, EMBED), BF16), shape((WIDTH, 8), I32)),
            in_specs=vmem(4) + [anywhere],
            out_specs=tuple(vmem(4)),
            compiler_params=params(),
            name="transpose_weights",
        )(w_in, w_mid, w_out, hash_seeds, send)
        own, one, two, three = pl.pallas_call(
            join_kernel,
            out_shape=(shape((512, EMBED), F32),) + (shape((512, EMBED), BF16),) * 3,
            in_specs=vmem(2) + [anywhere],
            out_specs=tuple(vmem(4)),
            compiler_params=params(),
            name="join_cores",
        )(keep, got, seeds_t)
        parts = [lax.ppermute(part, "z", shift(step)) for step, part in ((2, two), (1, one), (3, three))]

    slope_one, slope_two, own_units, send_units, other_enc = pl.pallas_call(
        forward_kernel,
        out_shape=(shape((WIDTH, SHARE), F32),) * 2 + (
            shape((3 * 512, SHARE), BF16), shape((2 * 512, SHARE), BF16), shape((512, SHARE), BF16)),
        in_specs=vmem(1) + [anywhere] + vmem(3),
        out_specs=tuple(vmem(5)),
        scratch_shapes=[pltpu.VMEM((8, WIDTH), I32)] + [pltpu.VMEM((WIDTH, SHARE), BF16)] * 3,
        compiler_params=params(),
        cost_estimate=pl.CostEstimate(flops=4 * 1024 ** 3, bytes_accessed=1 << 24, transcendentals=1 << 21),
        name="forward",
    )(table, one, seeds_t, w_in_t, w_mid_t)
    got_units = lax.ppermute(send_units, "core", SWAP)

    with jax.named_scope("grad_use"):
        grads = pl.pallas_call(
            total_kernel,
            out_shape=shape((SHARE, EMBED), BF16),
            in_specs=vmem(4) + [anywhere],
            out_specs=vmem(1)[0],
            compiler_params=params(),
            name="total_grads",
        )(own, *parts, own_units)

    with jax.named_scope("backward"):
        delta_two = pl.pallas_call(
            delta_two_kernel,
            out_shape=shape((1152, SHARE), BF16),
            in_specs=vmem(3),
            out_specs=vmem(1)[0],
            compiler_params=params(),
            name="delta_two",
        )(grads, slope_two, w_out)
        got_delta_two = lax.ppermute(delta_two, "core", SWAP)
        delta_one = pl.pallas_call(
            delta_one_kernel,
            out_shape=shape((WIDTH, SHARE), BF16),
            in_specs=vmem(3),
            out_specs=vmem(1)[0],
            compiler_params=params(),
            cost_estimate=pl.CostEstimate(flops=20 * 1024 ** 3, bytes_accessed=1 << 25, transcendentals=0),
            name="delta_one",
        )(delta_two, slope_one, w_mid)
        got_delta_one = lax.ppermute(delta_one, "core", SWAP)

    with jax.named_scope("sum_devices"):
        keep_two, *pieces = pl.pallas_call(
            weights_two_kernel,
            out_shape=(shape((128, 1024), F32),) + (shape((128, 1024), BF16),) * 3,
            in_specs=vmem(4),
            out_specs=tuple(vmem(4)),
            scratch_shapes=[pltpu.VMEM((512, 1024), F32)],
            compiler_params=params(),
            name="weights_two",
        )(own_units, delta_two, got_units, got_delta_two)
        rows_two = [lax.ppermute(pieces[step - 1], "z", shift(step)) for step in (2, 1, 3)]
        out_one = pl.pallas_call(
            weights_one_kernel,
            out_shape=shape((512, 1152), BF16),
            in_specs=vmem(7) + [anywhere],
            out_specs=anywhere,
            scratch_shapes=[pltpu.VMEM((512, 1152), BF16), pltpu.SemaphoreType.DMA((5,))],
            compiler_params=params(),
            name="weights_one",
        )(own_units, delta_one, other_enc, got_delta_one, delta_two, got_units, got_delta_two, pieces[0])
        columns_one = lax.all_to_all(out_one, ("x", "y"), split_axis=0, concat_axis=0, tiled=True)
        out_two = pl.pallas_call(
            sum_rows_kernel,
            out_shape=shape((128, 1024), BF16),
            in_specs=vmem(4),
            out_specs=vmem(1)[0],
            compiler_params=params(),
            name="sum_rows",
        )(keep_two, *rows_two)
        keep_one, *pieces = pl.pallas_call(
            sum_columns_kernel,
            out_shape=(shape((8, 1152), F32),) * 4,
            in_specs=vmem(1) + [anywhere],
            out_specs=tuple(vmem(4)),
            scratch_shapes=[pltpu.VMEM((32, 1152), F32)],
            compiler_params=params(),
            name="sum_columns",
        )(columns_one, out_two)
        rows_one = [lax.ppermute(pieces[step - 1], "z", shift(step)) for step in (2, 1, 3)]
        columns_two = lax.all_to_all(out_two, ("x", "y"), split_axis=0, concat_axis=0, tiled=True)
        return pl.pallas_call(
            last_kernel,
            out_shape=(shape((8, 1024), F32), shape((8, 1024), F32), shape((8, EMBED), F32)),
            in_specs=vmem(5),
            out_specs=tuple(vmem(3)),
            compiler_params=params(),
            name="last_sums",
        )(keep_one, *rows_one, columns_two)


def solution(mesh):
    fine = Mesh(mesh.devices.reshape(4, 2, 4, 4), ALL)
    split = P(ALL)
    rows = P(ALL, None)
    return jax.shard_map(
        per_device, mesh=fine, in_specs=(rows, split, split, split, split, P(), P(), P(), P()),
        out_specs=(rows, rows, rows), check_vma=False)
```
